32 devices in a mesh: groups: 2 (over x), tm: 16 (over z, y, core).
Axes of the slice: x: 2, y: 2, z: 4, core: 2. Of those that a mesh axis runs over, the one named last changes fastest.
Arguments:
- signal: float32 [2, 8192], P('groups', 'tm'), parts along dimension 0, may hold values from -6 to 6
- codes: bfloat16 [2, 1024, 8192], P('groups', None, 'tm'), parts along dimension 0, may hold values from -6 to 6
- dictionary: float32 [1024, 512], P('tm'), may hold values from -6 to 6
- thresholds: float32 [1024], replicated, may hold values from 0.02 to 0.2
Outputs:
- codes_out: bfloat16 [2, 1024, 8192], P('groups', None, 'tm'), parts along dimension 0
- dictionary_out: float32 [2048, 512], P(('groups', 'tm')), parts along dimension 0
- residual_out: float32 [2, 8192], P('groups', 'tm'), parts along dimension 0
The draws below stay inside these ranges and needn't reach their ends.
There are 2 independent parts, one for each index of `groups`. The reference program is written for one: setup_inputs(seed, part) draws one part's arguments, and reference() takes and returns one part's arrays. A program takes and returns all parts, laid end to end along the dimension named above; an argument that names none is the same for every part. Nothing has to cross between parts.
All inputs are finite; a program needn't handle non-finite values.
Results may differ from the reference program's by a relative error of at most 0.0072.
Values may be sent and summed in bfloat16 or wider, within the bound.
No kernel may reach another device: no remote copies, remote signals or barrier semaphores. Data moves between devices by JAX's collectives and lax.ppermute only.
A program may use at most 64 MiB of HBM per device.

```python
import math
import jax
import jax.numpy as jnp
from jax import lax

C = 1
K = 1024
L = 512
ITERS = 2
T_SIZE = 8192


def raised(values, key, source, target, parts, factor):
    def block_of(axis_at):
        return (jnp.arange(values.shape[axis_at]) // (values.shape[axis_at] // parts)).reshape((-1,) + (1,) * (values.ndim - 1 - axis_at))

    near = jax.random.permutation(key, parts)[block_of(target)]
    second = (block_of(target) + parts // 2) % parts
    return jnp.where((block_of(source) == near) | (block_of(source) == second), factor * values, values)


def level_of(key, shape, shards, low, high):
    level, own = 1.0, jax.random.fold_in(key, 6)
    for dim, shards_of in shards:
        steps = jnp.exp(jax.random.uniform(jax.random.fold_in(own, dim), (shards_of,), jnp.float32, low / len(shards), high / len(shards)))
        level = level * jnp.repeat(steps, shape[dim] // shards_of).reshape([-1 if axis == dim else 1 for axis in range(len(shape))])
    return level


def scatter_about(key, extent, deviation, most, shards=(), kind=jnp.bfloat16):
    level = level_of(key, extent, shards, -0.22, 0.18) if shards else 1.0
    values = jax.random.normal(key, extent, jnp.float32) * deviation * level
    return jnp.minimum(jnp.maximum(values, -most), most).astype(kind)


def noise_with(key, extent, width, limit, pieces, heavy, dtype=jnp.bfloat16):
    drawn = width * jax.random.normal(key, extent, jnp.float32)
    if pieces:
        drawn = drawn * level_of(key, extent, pieces, -0.22, 0.18)
    return jnp.clip(raised(drawn, jax.random.fold_in(key, 3), *heavy), -limit, limit).astype(dtype)


def setup_inputs(seed: int = 0, part: int = 0) -> dict:
    keys = jax.random.split(jax.random.key(seed), 5)
    own_keys = jax.random.split(jax.random.fold_in(keys[4], part), 5)
    signal = scatter_about(own_keys[0], (C, T_SIZE), 1.0, 6.0, ((1, 16),), jnp.float32)
    codes = noise_with(own_keys[1], (C, K, T_SIZE), 1.0, 6.0, ((2, 16),), (2, 1, 16, 2.0))
    dictionary = scatter_about(keys[2], (K, L), 1.0, 6.0, ((0, 16),), jnp.float32)
    thresholds = jnp.clip(jnp.exp(jax.random.uniform(keys[3], (K,), jnp.float32, math.log(0.02), math.log(0.2))), 0.02, 0.2)
    return {"signal": signal, "codes": codes, "dictionary": dictionary, "thresholds": thresholds}


CODE_STEP = 6.0
EPSILON = 1e-06

def round_keep(values):
    return lax.optimization_barrier(values.astype(jnp.bfloat16)).astype(jnp.float32)

def reference(signal, codes, dictionary, thresholds):
    factor = (K * L) ** (-0.5)
    current = codes.astype(jnp.float32)
    atoms_now = dictionary
    residual = signal
    numbers = ('NCH', 'OIH', 'NCH')
    for iteration in range(ITERS):
        dict_b = round_keep(atoms_now)
        codes_b = round_keep(current)
        rebuilt = lax.conv_general_dilated(codes_b, dict_b[None, :, ::-1], (1,), [(L - 1, 0)], dimension_numbers=numbers, precision=lax.Precision.HIGHEST)[:, 0, :]
        residual = signal - factor * rebuilt
        rounded = round_keep(residual)
        matched = lax.conv_general_dilated(rounded[:, None, :], dict_b[:, None, :], (1,), [(0, L - 1)], dimension_numbers=numbers, precision=lax.Precision.HIGHEST)
        gradient = factor * lax.conv_general_dilated(rounded[None], jnp.transpose(codes_b, (1, 0, 2)), (1,), [(0, L - 1)], dimension_numbers=numbers, precision=lax.Precision.HIGHEST)[0]
        shrink = current + CODE_STEP * factor * matched
        cutoff = CODE_STEP * thresholds[None, :, None]
        current = jnp.sign(shrink) * jnp.maximum(jnp.abs(shrink) - cutoff, 0.0)
        updated = atoms_now + gradient
        atoms_now = updated / jnp.sqrt(lax.optimization_barrier(jnp.mean(updated * updated, axis=1, keepdims=True)) + EPSILON)
    return (current.astype(jnp.bfloat16), atoms_now, residual)
```

```python
import functools

import jax
import jax.numpy as jnp
from jax import lax
from jax.experimental import pallas as pl
from jax.experimental.pallas import tpu as pltpu
from jax.sharding import PartitionSpec as P

CODE_STEP = 6.0
EPSILON = 1e-06
LANES = 128
F32, BF16 = jnp.float32, jnp.bfloat16
VMEM_BYTES = 48 * 1024 * 1024


def dot(a, b, dims):
    return lax.dot_general(a, b, (dims, ((), ())), preferred_element_type=F32)


def repeat(count, body):
    if count <= 16:
        for i in range(count):
            body(i)
    else:
        def step(i, carry):
            body(i)
            return carry
        lax.fori_loop(0, count, step, 0)


def row_lane():
    shape = (LANES, LANES)
    return lax.broadcasted_iota(jnp.int32, shape, 0), lax.broadcasted_iota(jnp.int32, shape, 1)


def turned_left(row):
    group = jnp.broadcast_to(row, (8, LANES))
    q = lax.broadcasted_iota(jnp.int32, (8, LANES), 0)
    for bit in (1, 2, 4):
        group = jnp.where((q & bit) != 0, pltpu.roll(group, LANES - bit, 1), group)
    return jnp.concatenate([group] + [pltpu.roll(group, LANES - a, 1) for a in range(8, LANES, 8)], axis=0)


def fill_hankel(rows_ref, hankel_ref, first, count):
    q, v = row_lane()
    keep = q + v < LANES
    here = turned_left(rows_ref[pl.ds(first, 1), :])
    for i in range(count):
        after = turned_left(rows_ref[pl.ds(first + i + 1, 1), :])
        hankel_ref[first + i] = jnp.where(keep, here, after).astype(BF16)
        here = after


def windows_of(hankel_ref, slab, width):
    per = width // LANES
    rows = [
        jnp.concatenate([hankel_ref[slab * per + p + i] for i in range(per)], axis=1)
        for p in range(per)
    ]
    return jnp.concatenate(rows, axis=0)


def soft(value, cutoff):
    return value - jnp.minimum(jnp.maximum(value, -cutoff), cutoff)


def normalised(updated):
    return updated / jnp.sqrt(jnp.mean(updated * updated, axis=1, keepdims=True) + EPSILON)


def stacked_taps(atoms):
    return jnp.concatenate([atoms[:, i : i + LANES] for i in range(0, atoms.shape[1], LANES)], axis=0)


def rebuild(taps, slab_of, slabs, width, turned_ref, sums_ref):
    per = width // LANES
    q, v = row_lane()
    keep = v >= q
    turned_ref[...] = jnp.zeros_like(turned_ref)

    def body(n):
        now, before = slab_of(n), slab_of(n - 1)
        shifted = [now] + [
            jnp.concatenate([before[:, width - LANES * p :], now[:, : width - LANES * p]], axis=1) for p in range(1, per)
        ]
        products = dot(taps, jnp.concatenate(shifted, axis=0), ((0,), (0,)))
        last = turned_ref[...]
        for i in range(per):
            turned = pltpu.roll(products[:, LANES * i : LANES * (i + 1)], 0, 1, stride=1, stride_axis=0)
            placed = jnp.where(keep, turned, last)
            sums_ref[n * per + i] = placed.reshape(LANES // 8, 8, LANES).sum(axis=0)
            last = turned
        turned_ref[...] = last

    repeat(slabs, body)


def partial_residual(me, factor, signal_ref, sums_ref, out_ref):
    rows = signal_ref.shape[0]
    out_ref[...] = -factor * jnp.sum(sums_ref[...], axis=1)
    own = pl.ds(me * rows, rows)
    out_ref[own, :] = out_ref[own, :] + signal_ref[...]


def first_kernel(factor, me_ref, atoms_ref, codes_ref, signal_ref, out_ref, turned_ref, sums_ref):
    slabs, owned, width = codes_ref.shape
    taps = stacked_taps(atoms_ref[...].astype(BF16))
    zero = jnp.zeros((owned, width), BF16)

    def slab_of(n):
        if isinstance(n, int):
            return codes_ref[n] if n >= 0 else zero
        return jnp.where(n >= 0, codes_ref[jnp.maximum(n, 0)], zero)

    rebuild(taps, slab_of, slabs, width, turned_ref, sums_ref)
    partial_residual(me_ref[0], factor, signal_ref, sums_ref, out_ref)


def round_rows(residual_ref, rows_ref):
    count = residual_ref.shape[0]
    rows_ref[:count, :] = residual_ref[...].astype(BF16).astype(F32)
    rows_ref[count:, :] = jnp.zeros((rows_ref.shape[0] - count, LANES), F32)


def second_kernel(
    factor, me_ref, residual_ref, atoms_ref, codes_ref, thresholds_ref, signal_ref,
    atoms_out, rounded_out, codes_out, part_out,
    rows_ref, hankel_ref, gradient_ref, turned_ref, sums_ref,
):
    slabs, owned, width = codes_ref.shape
    per = width // LANES
    round_rows(residual_ref, rows_ref)
    atoms = atoms_ref[...]
    atoms_b = atoms.astype(BF16)
    cutoff = CODE_STEP * thresholds_ref[...]
    gradient_ref[...] = jnp.zeros_like(gradient_ref)
    codes_out[0] = jnp.zeros((owned, width), BF16)
    fill_hankel(rows_ref, hankel_ref, 0, per - 1)

    def body(n):
        fill_hankel(rows_ref, hankel_ref, n * per + per - 1, per)
        frames = windows_of(hankel_ref, n, width)
        code = codes_ref[n]
        both = dot(jnp.concatenate([atoms_b, code], axis=0), frames, ((1,), (0,)))
        gradient_ref[...] += both[owned:]
        value = code.astype(F32) + (CODE_STEP * factor) * both[:owned]
        codes_out[n + 1] = soft(value, cutoff).astype(BF16)

    repeat(slabs, body)
    after = normalised(atoms + factor * gradient_ref[...])
    atoms_out[...] = after
    after_b = after.astype(BF16)
    rounded_out[...] = after_b
    rebuild(stacked_taps(after_b), lambda n: codes_out[n + 1], slabs, width, turned_ref, sums_ref)
    partial_residual(me_ref[0], factor, signal_ref, sums_ref, part_out)


def third_kernel(
    factor, me_ref, first_ref, second_ref, atoms_ref, owned_codes_ref, before_ref, after_ref, codes_ref, thresholds_ref,
    atoms_out, residual_out, codes_out,
    rows_ref, hankel_ref, gradient_ref, part_rows_ref, part_hankel_ref,
):
    slabs, owned, width = owned_codes_ref.shape
    slabs -= 1
    per = width // LANES
    me = me_ref[0]
    cutoff = CODE_STEP * thresholds_ref[...]
    frames = []
    for i, residual in enumerate((first_ref, second_ref)):
        round_rows(residual, rows_ref)
        part_rows_ref[: 2 * per, :] = rows_ref[pl.ds(me * per, 2 * per), :]
        fill_hankel(part_rows_ref, part_hankel_ref, 0, 2 * per - 1)
        frames.append(windows_of(part_hankel_ref, 0, width))
    step = 256 if codes_ref.shape[0] % 256 == 0 else codes_ref.shape[0]
    for start in range(0, codes_ref.shape[0], step):
        own = slice(start, start + step)
        value = codes_ref[own, :].astype(F32)
        for atoms_b, frame in ((before_ref, frames[0]), (after_ref, frames[1])):
            value = soft(value + (CODE_STEP * factor) * dot(atoms_b[own, :], frame, ((1,), (0,))), cutoff[own, :])
        codes_out[own, :] = value.astype(BF16)
    gradient_ref[...] = jnp.zeros_like(gradient_ref)
    fill_hankel(rows_ref, hankel_ref, 0, per - 1)

    def body(n):
        fill_hankel(rows_ref, hankel_ref, n * per + per - 1, per)
        gradient_ref[...] += dot(owned_codes_ref[n + 1], windows_of(hankel_ref, n, width), ((1,), (0,)))

    repeat(slabs, body)
    atoms_out[...] = normalised(atoms_ref[...] + factor * gradient_ref[...])
    residual_out[...] = second_ref[pl.ds(me * per, per), :]


def call(kernel, outs, scratch, *args):
    vmem = pl.BlockSpec(memory_space=pltpu.VMEM)
    return pl.pallas_call(
        kernel,
        out_shape=outs,
        in_specs=[pl.BlockSpec(memory_space=pltpu.SMEM)] + [vmem] * (len(args) - 1),
        out_specs=jax.tree.map(lambda _: vmem, outs),
        scratch_shapes=scratch,
        compiler_params=pltpu.CompilerParams(vmem_limit_bytes=VMEM_BYTES),
    )(*args)


def swapped(block, distance):
    count = lax.axis_size("tm")
    return lax.ppermute(block, "tm", [(i, i ^ distance) for i in range(count)])


def gathered(block):
    me = lax.axis_index("tm")
    rows, width = block.shape
    block = block[None]
    distance = lax.axis_size("tm") // 2
    while distance:
        other = swapped(block, distance)
        upper = (me & distance) != 0
        low, high = jnp.where(upper, other, block), jnp.where(upper, block, other)
        block = jnp.stack([low, high], axis=1).reshape(-1, rows, width)
        distance //= 2
    return block.reshape(-1, width)


def summed(part):
    distance = 1
    while distance < lax.axis_size("tm"):
        part = part + swapped(part, distance)
        distance *= 2
    return part


def on_device(signal, codes, dictionary, thresholds):
    _, atom_count, width = codes.shape
    owned, lag_count = dictionary.shape
    slabs = lax.axis_size("tm")
    per = width // LANES
    blocks = slabs * per
    factor = (atom_count * lag_count) ** (-0.5)
    me = lax.axis_index("tm")
    at = me.astype(jnp.int32).reshape(1)
    signal_rows = signal.reshape(per, LANES)
    own_thresholds = lax.dynamic_slice(thresholds, (me * owned,), (owned,)).reshape(owned, 1)
    codes = codes[0]

    by_atom = lax.all_to_all(codes.reshape(slabs, owned, width), "tm", 0, 0, tiled=True)
    before = gathered(dictionary.astype(BF16))

    sums = [pltpu.VMEM((LANES, LANES), F32), pltpu.VMEM((blocks, 8, LANES), F32)]
    rows = [
        pltpu.VMEM((blocks + 8, LANES), F32),
        pltpu.VMEM((blocks + per - 1, LANES, LANES), BF16),
        pltpu.VMEM((owned, lag_count), F32),
    ]
    residual_shape = jax.ShapeDtypeStruct((blocks, LANES), F32)
    part = call(functools.partial(first_kernel, factor), residual_shape, sums, at, dictionary, by_atom, signal_rows)
    first = summed(part)
    atoms, after, next_codes, part = call(
        functools.partial(second_kernel, factor),
        (
            jax.ShapeDtypeStruct((owned, lag_count), F32),
            jax.ShapeDtypeStruct((owned, lag_count), BF16),
            jax.ShapeDtypeStruct((slabs + 1, owned, width), BF16),
            residual_shape,
        ),
        rows + sums,
        at, first, dictionary, by_atom, own_thresholds, signal_rows,
    )
    second = summed(part)
    after = gathered(after)
    atoms, residual, codes = call(
        functools.partial(third_kernel, factor),
        (
            jax.ShapeDtypeStruct((owned, lag_count), F32),
            jax.ShapeDtypeStruct((per, LANES), F32),
            jax.ShapeDtypeStruct((atom_count, width), BF16),
        ),
        rows + [pltpu.VMEM((2 * per, LANES), F32), pltpu.VMEM((2 * per - 1, LANES, LANES), BF16)],
        at, first, second, atoms, next_codes, before, after, codes, thresholds.reshape(atom_count, 1),
    )
    return codes[None], atoms, residual.reshape(1, width)


def solution(mesh):
    return jax.shard_map(
        on_device,
        mesh=mesh,
        in_specs=(P("groups", "tm"), P("groups", None, "tm"), P("tm", None), P()),
        out_specs=(P("groups", None, "tm"), P(("groups", "tm"), None), P("groups", "tm")),
        check_vma=False,
    )
```

```python
import functools

import jax
import jax.numpy as jnp
from jax import lax
from jax.experimental import pallas as pl
from jax.experimental.pallas import tpu as pltpu
from jax.sharding import PartitionSpec as P

CODE_STEP = 6.0
EPSILON = 1e-06
LANES = 128
F32, BF16 = jnp.float32, jnp.bfloat16
VMEM_BYTES = 48 * 1024 * 1024


def dot(a, b, dims):
    return lax.dot_general(a, b, (dims, ((), ())), preferred_element_type=F32)


def repeat(count, body):
    if count <= 16:
        for i in range(count):
            body(i)
    else:
        def step(i, carry):
            body(i)
            return carry
        lax.fori_loop(0, count, step, 0)


def row_lane():
    shape = (LANES, LANES)
    return lax.broadcasted_iota(jnp.int32, shape, 0), lax.broadcasted_iota(jnp.int32, shape, 1)


def turned_left(row):
    group = jnp.broadcast_to(row, (8, LANES))
    q = lax.broadcasted_iota(jnp.int32, (8, LANES), 0)
    for bit in (1, 2, 4):
        group = jnp.where((q & bit) != 0, pltpu.roll(group, LANES - bit, 1), group)
    return jnp.concatenate([group] + [pltpu.roll(group, LANES - a, 1) for a in range(8, LANES, 8)], axis=0)


def fill_hankel(rows_ref, hankel_ref, first, count):
    q, v = row_lane()
    keep = q + v < LANES
    here = turned_left(rows_ref[pl.ds(first, 1), :])
    for i in range(count):
        after = turned_left(rows_ref[pl.ds(first + i + 1, 1), :])
        hankel_ref[first + i] = jnp.where(keep, here, after).astype(BF16)
        here = after


def windows_of(hankel_ref, slab, width):
    per = width // LANES
    rows = [
        jnp.concatenate([hankel_ref[slab * per + p + i] for i in range(per)], axis=1)
        for p in range(per)
    ]
    return jnp.concatenate(rows, axis=0)


def soft(value, cutoff):
    return value - jnp.minimum(jnp.maximum(value, -cutoff), cutoff)


def normalised(updated):
    return updated / jnp.sqrt(jnp.mean(updated * updated, axis=1, keepdims=True) + EPSILON)


def stacked_taps(atoms):
    return jnp.concatenate([atoms[:, i : i + LANES] for i in range(0, atoms.shape[1], LANES)], axis=0)


def rebuild(taps, slab_of, slabs, width, turned_ref, sums_ref):
    per = width // LANES
    q, v = row_lane()
    keep = v >= q
    turned_ref[...] = jnp.zeros_like(turned_ref)

    def body(n):
        now, before = slab_of(n), slab_of(n - 1)
        shifted = [now] + [
            jnp.concatenate([before[:, width - LANES * p :], now[:, : width - LANES * p]], axis=1) for p in range(1, per)
        ]
        products = dot(taps, jnp.concatenate(shifted, axis=0), ((0,), (0,)))
        last = turned_ref[...]
        for i in range(per):
            turned = pltpu.roll(products[:, LANES * i : LANES * (i + 1)], 0, 1, stride=1, stride_axis=0)
            placed = jnp.where(keep, turned, last)
            sums_ref[n * per + i] = placed.reshape(LANES // 8, 8, LANES).sum(axis=0)
            last = turned
        turned_ref[...] = last

    repeat(slabs, body)


def partial_residual(me, factor, signal_ref, sums_ref, out_ref):
    rows = signal_ref.shape[0]
    out_ref[...] = -factor * jnp.sum(sums_ref[...], axis=1)
    own = pl.ds(me * rows, rows)
    out_ref[own, :] = out_ref[own, :] + signal_ref[...]


def owner_of(me, place, count):
    distance, bit = count // 2, 0
    while distance:
        if place >> bit & 1:
            me = me ^ distance
        distance, bit = distance // 2, bit + 1
    return me


def first_kernel(factor, me_ref, near_ref, far_ref, codes_ref, signal_ref, out_ref):
    half, owned, lag_count = near_ref.shape
    width = codes_ref.shape[1]
    per, reach = width // LANES, lag_count // LANES
    me = me_ref[0]
    together = max(1, min(half, 256 // owned))
    lagged = jnp.zeros((lag_count, width), F32)
    for side, ref in enumerate((near_ref, far_ref)):
        for start in range(0, half, together):
            places = range(start, start + together)
            code = [codes_ref[pl.ds(pl.multiple_of(owner_of(me, side * half + b, 2 * half) * owned, owned), owned), :] for b in places]
            atoms = [ref[b] for b in places]
            lagged = lagged + dot(jnp.concatenate(atoms, axis=0), jnp.concatenate(code, axis=0), ((0,), (0,)))
    q, v = row_lane()
    keep = v >= q
    last = jnp.zeros((LANES, LANES), F32)
    for m in range(per + reach):
        pieces = [
            lagged[LANES * p : LANES * (p + 1), LANES * (m - p) : LANES * (m - p + 1)] for p in range(reach) if 0 <= m - p < per
        ]
        turned = jnp.zeros((LANES, LANES), F32)
        if pieces:
            turned = pltpu.roll(sum(pieces[1:], pieces[0]), 0, 1, stride=1, stride_axis=0)
        row = -factor * jnp.sum(jnp.where(keep, turned, last), axis=0, keepdims=True)
        out_ref[m : m + 1, :] = row + signal_ref[m : m + 1, :] if m < per else row
        last = turned


def round_rows(residual_ref, count, rows_ref):
    rows_ref[:count, :] = residual_ref[:count, :].astype(BF16).astype(F32)
    rows_ref[count:, :] = jnp.zeros((rows_ref.shape[0] - count, LANES), F32)


def second_kernel(
    factor, me_ref, near_ref, far_ref, atoms_ref, codes_ref, thresholds_ref, signal_ref,
    atoms_out, taps_out, codes_out, part_out, rows_ref,
    hankel_ref, gradient_ref, turned_ref, sums_ref,
):
    slabs, owned, width = codes_ref.shape
    per = width // LANES
    half, span, _ = near_ref.shape
    rows_ref[...] = jnp.zeros_like(rows_ref)
    for side, ref in enumerate((near_ref, far_ref)):
        for b in range(half):
            there = pl.ds(owner_of(me_ref[0], side * half + b, slabs) * per, span)
            rows_ref[there, :] = rows_ref[there, :] + ref[b]
    round_rows(rows_ref, slabs * per, rows_ref)
    atoms = atoms_ref[...]
    atoms_b = atoms.astype(BF16)
    cutoff = CODE_STEP * thresholds_ref[...]
    gradient_ref[...] = jnp.zeros_like(gradient_ref)
    codes_out[0] = jnp.zeros((owned, width), BF16)
    fill_hankel(rows_ref, hankel_ref, 0, per - 1)

    def body(n):
        fill_hankel(rows_ref, hankel_ref, n * per + per - 1, per)
        frames = windows_of(hankel_ref, n, width)
        code = codes_ref[n]
        both = dot(jnp.concatenate([atoms_b, code], axis=0), frames, ((1,), (0,)))
        gradient_ref[...] += both[owned:]
        value = code.astype(F32) + (CODE_STEP * factor) * both[:owned]
        codes_out[n + 1] = soft(value, cutoff).astype(BF16)

    repeat(slabs, body)
    after = normalised(atoms + factor * gradient_ref[...])
    atoms_out[...] = after
    after_b = after.astype(BF16)
    taps = stacked_taps(after_b)
    taps_out[...] = taps
    rebuild(taps, lambda n: codes_out[n + 1], slabs, width, turned_ref, sums_ref)
    partial_residual(me_ref[0], factor, signal_ref, sums_ref, part_out)


def third_kernel(
    factor, me_ref, first_ref, second_ref, atoms_ref, owned_codes_ref,
    near_before_ref, far_before_ref, near_after_ref, far_after_ref, codes_ref, thresholds_ref,
    atoms_out, residual_out, codes_out,
    rows_ref, hankel_ref, gradient_ref, part_rows_ref, part_hankel_ref,
):
    slabs, owned, width = owned_codes_ref.shape
    slabs -= 1
    per, half = width // LANES, slabs // 2
    reach = near_before_ref.shape[2] // LANES
    me = me_ref[0]
    round_rows(second_ref, slabs * per, rows_ref)
    frames = []
    for residual in (first_ref, rows_ref):
        part_rows_ref[: 2 * per, :] = residual[pl.ds(me * per, 2 * per), :]
        fill_hankel(part_rows_ref, part_hankel_ref, 0, 2 * per - 1)
        frames.append(windows_of(part_hankel_ref, 0, width))
    together = max(1, min(half, 256 // owned))
    for side, before, after in ((0, near_before_ref, near_after_ref), (1, far_before_ref, far_after_ref)):
        for start in range(0, half, together):
            places = range(start, start + together)
            there = [pl.ds(pl.multiple_of(owner_of(me, side * half + b, slabs) * owned, owned), owned) for b in places]
            value = jnp.concatenate([codes_ref[own, :] for own in there], axis=0).astype(F32)
            cutoff = jnp.concatenate([CODE_STEP * thresholds_ref[own, :] for own in there], axis=0)
            old = jnp.concatenate([before[b] for b in places], axis=0)
            new = jnp.concatenate(
                [
                    jnp.concatenate([after[(b * reach + p) * owned : (b * reach + p + 1) * owned, :] for p in range(reach)], axis=1)
                    for b in places
                ],
                axis=0,
            )
            for atoms_b, frame in ((old, frames[0]), (new, frames[1])):
                value = soft(value + (CODE_STEP * factor) * dot(atoms_b, frame, ((1,), (0,))), cutoff)
            value = value.astype(BF16)
            for i, own in enumerate(there):
                codes_out[own, :] = value[i * owned : (i + 1) * owned]
    gradient_ref[...] = jnp.zeros_like(gradient_ref)
    fill_hankel(rows_ref, hankel_ref, 0, per - 1)

    def body(n):
        fill_hankel(rows_ref, hankel_ref, n * per + per - 1, per)
        gradient_ref[...] += dot(owned_codes_ref[n + 1], windows_of(hankel_ref, n, width), ((1,), (0,)))

    repeat(slabs, body)
    atoms_out[...] = normalised(atoms_ref[...] + factor * gradient_ref[...])
    residual_out[...] = second_ref[pl.ds(me * per, per), :]


def call(kernel, outs, scratch, *args):
    vmem = pl.BlockSpec(memory_space=pltpu.VMEM)
    return pl.pallas_call(
        kernel,
        out_shape=outs,
        in_specs=[pl.BlockSpec(memory_space=pltpu.SMEM)] + [vmem] * (len(args) - 1),
        out_specs=jax.tree.map(lambda _: vmem, outs),
        scratch_shapes=scratch,
        compiler_params=pltpu.CompilerParams(vmem_limit_bytes=VMEM_BYTES),
    )(*args)


def swapped(block, distance):
    count = lax.axis_size("tm")
    return lax.ppermute(block, "tm", [(i, i ^ distance) for i in range(count)])


def gathered(block):
    block = block[None]
    distance = lax.axis_size("tm") // 2
    while True:
        other = swapped(block, distance)
        if distance == 1:
            return block, other
        block = jnp.concatenate([block, other])
        distance //= 2


def gathered_and_summed(block, part):
    distance = lax.axis_size("tm") // 2
    rows = part.shape[0]
    while True:
        high = lax.reduce_precision(part, 8, 7)
        low = lax.reduce_precision(part - high, 8, 7)
        mine = jnp.concatenate([block, high.astype(BF16), low.astype(BF16)])
        other = swapped(mine, distance)
        end = block.shape[0]
        part = (high + low) + (other[end : end + rows].astype(F32) + other[end + rows :].astype(F32))
        if distance == 1:
            return mine, other, part
        block = jnp.concatenate([block, other[:end]])
        distance //= 2


def on_device(signal, codes, dictionary, thresholds):
    _, atom_count, width = codes.shape
    owned, lag_count = dictionary.shape
    slabs = lax.axis_size("tm")
    per = width // LANES
    blocks = slabs * per
    factor = (atom_count * lag_count) ** (-0.5)
    me = lax.axis_index("tm")
    at = me.astype(jnp.int32).reshape(1)
    signal_rows = signal.reshape(per, LANES)
    own_thresholds = lax.dynamic_slice(thresholds, (me * owned,), (owned,)).reshape(owned, 1)
    codes = codes[0]

    near_before, far_before = gathered(dictionary.astype(BF16))
    by_atom = lax.all_to_all(codes.reshape(slabs, owned, width), "tm", 0, 0, tiled=True)

    part = call(
        functools.partial(first_kernel, factor),
        jax.ShapeDtypeStruct((per + lag_count // LANES, LANES), F32),
        [],
        at, near_before, far_before, codes, signal_rows,
    )
    near, far = gathered(part)
    hankel = [pltpu.VMEM((blocks + per - 1, LANES, LANES), BF16), pltpu.VMEM((owned, lag_count), F32)]
    atoms, taps, next_codes, part, first = call(
        functools.partial(second_kernel, factor),
        (
            jax.ShapeDtypeStruct((owned, lag_count), F32),
            jax.ShapeDtypeStruct((owned * lag_count // LANES, LANES), BF16),
            jax.ShapeDtypeStruct((slabs + 1, owned, width), BF16),
            jax.ShapeDtypeStruct((blocks, LANES), F32),
            jax.ShapeDtypeStruct((blocks + 8, LANES), F32),
        ),
        hankel + [pltpu.VMEM((LANES, LANES), F32), pltpu.VMEM((blocks, 8, LANES), F32)],
        at, near, far, dictionary, by_atom, own_thresholds, signal_rows,
    )
    near_after, far_after, second = gathered_and_summed(taps, part)
    atoms, residual, codes = call(
        functools.partial(third_kernel, factor),
        (
            jax.ShapeDtypeStruct((owned, lag_count), F32),
            jax.ShapeDtypeStruct((per, LANES), F32),
            jax.ShapeDtypeStruct((atom_count, width), BF16),
        ),
        [pltpu.VMEM((blocks + 8, LANES), F32)]
        + hankel
        + [pltpu.VMEM((2 * per, LANES), F32), pltpu.VMEM((2 * per - 1, LANES, LANES), BF16)],
        at, first, second, atoms, next_codes,
        near_before, far_before, near_after, far_after, codes, thresholds.reshape(atom_count, 1),
    )
    return codes[None], atoms, residual.reshape(1, width)


def solution(mesh):
    return jax.shard_map(
        on_device,
        mesh=mesh,
        in_specs=(P("groups", "tm"), P("groups", None, "tm"), P("tm", None), P()),
        out_specs=(P("groups", None, "tm"), P(("groups", "tm"), None), P("groups", "tm")),
        check_vma=False,
    )
```

```python
import functools

import jax
import jax.numpy as jnp
from jax import lax
from jax.experimental import pallas as pl
from jax.experimental.pallas import tpu as pltpu
from jax.sharding import PartitionSpec as P

CODE_STEP = 6.0
EPSILON = 1e-06
LANES = 128
F32, BF16 = jnp.float32, jnp.bfloat16
VMEM_BYTES = 48 * 1024 * 1024


def dot(a, b, dims):
    return lax.dot_general(a, b, (dims, ((), ())), preferred_element_type=F32)


def repeat(count, body, carry=None):
    def step(i, carry):
        return body(i) if carry is None else body(i, carry)

    if count > 80:
        return lax.fori_loop(0, count, step, carry)
    for i in range(count):
        carry = step(i, carry)
    return carry


def row_lane():
    shape = (LANES, LANES)
    return lax.broadcasted_iota(jnp.int32, shape, 0), lax.broadcasted_iota(jnp.int32, shape, 1)


def fill_hankel(rows_ref, turned_ref, hankel_ref):
    count = hankel_ref.shape[0]
    q = lax.broadcasted_iota(jnp.int32, (8, LANES), 0)
    v = lax.broadcasted_iota(jnp.int32, (8, LANES), 1)

    def turn(m):
        group = jnp.broadcast_to(rows_ref[pl.ds(m, 1), :], (8, LANES))
        for bit in (1, 2, 4):
            group = jnp.where((q & bit) != 0, pltpu.roll(group, LANES - bit, 1), group)
        turned_ref[m] = group

    repeat(count + 1, turn)
    for a in range(0, LANES, 16):
        keeps = [q + v + (a + b) < LANES for b in (0, 8)]

        def groups(m):
            group = turned_ref[m]
            return tuple(pltpu.roll(group, LANES - a - b, 1) if a + b else group for b in (0, 8))

        def place(m, here):
            after = groups(m + 1)
            pair = [jnp.where(keep, old, new) for keep, old, new in zip(keeps, here, after)]
            hankel_ref[m, a : a + 16, :] = jnp.concatenate(pair, axis=0).astype(BF16)
            return after

        repeat(count, place, groups(0))


def windows_of(hankel_ref, slab, width):
    per = width // LANES
    rows = [
        jnp.concatenate([hankel_ref[slab * per + p + i] for i in range(per)], axis=1)
        for p in range(per)
    ]
    return jnp.concatenate(rows, axis=0)


def soft(value, cutoff):
    return value - jnp.minimum(jnp.maximum(value, -cutoff), cutoff)


def normalised(updated):
    return updated / jnp.sqrt(jnp.mean(updated * updated, axis=1, keepdims=True) + EPSILON)


def stacked_taps(atoms):
    return jnp.concatenate([atoms[:, i : i + LANES] for i in range(0, atoms.shape[1], LANES)], axis=0)


def rebuild(taps, slab_of, slabs, width, turned_ref, sums_ref):
    per = width // LANES
    q, v = row_lane()
    keep = v >= q
    turned_ref[...] = jnp.zeros_like(turned_ref)

    def body(n):
        now, before = slab_of(n), slab_of(n - 1)
        shifted = [now] + [
            jnp.concatenate([before[:, width - LANES * p :], now[:, : width - LANES * p]], axis=1) for p in range(1, per)
        ]
        products = dot(taps, jnp.concatenate(shifted, axis=0), ((0,), (0,)))
        last = turned_ref[...]
        for i in range(per):
            turned = pltpu.roll(products[:, LANES * i : LANES * (i + 1)], 0, 1, stride=1, stride_axis=0)
            placed = jnp.where(keep, turned, last)
            sums_ref[n * per + i] = placed.reshape(LANES // 8, 8, LANES).sum(axis=0)
            last = turned
        turned_ref[...] = last

    repeat(slabs, body)


def partial_residual(me, factor, signal_ref, sums_ref, out_ref):
    rows = signal_ref.shape[0]
    out_ref[...] = -factor * jnp.sum(sums_ref[...], axis=1)
    own = pl.ds(me * rows, rows)
    out_ref[own, :] = out_ref[own, :] + signal_ref[...]


def owner_of(me, place, count):
    distance, bit = count // 2, 0
    while distance:
        if place >> bit & 1:
            me = me ^ distance
        distance, bit = distance // 2, bit + 1
    return me


def first_kernel(factor, me_ref, atoms_ref, codes_ref, signal_ref, taps_out, part_out, turned_ref, sums_ref):
    slabs, owned, width = codes_ref.shape
    taps = stacked_taps(atoms_ref[...].astype(BF16))
    taps_out[...] = taps
    zero = jnp.zeros((owned, width), BF16)

    def slab_of(n):
        if isinstance(n, int):
            return codes_ref[n] if n >= 0 else zero
        return jnp.where(n >= 0, codes_ref[jnp.maximum(n, 0)], zero)

    rebuild(taps, slab_of, slabs, width, turned_ref, sums_ref)
    partial_residual(me_ref[0], factor, signal_ref, sums_ref, part_out)


def round_rows(residual_ref, rows_ref):
    count = residual_ref.shape[0]
    rows_ref[:count, :] = residual_ref[...].astype(BF16).astype(F32)
    rows_ref[count:, :] = jnp.zeros((rows_ref.shape[0] - count, LANES), F32)


def second_kernel(
    factor, me_ref, residual_ref, atoms_ref, codes_ref, thresholds_ref, signal_ref,
    atoms_out, taps_out, codes_out, part_out, frames_out,
    rows_ref, turned_rows_ref, hankel_ref, gradient_ref, turned_ref, sums_ref,
):
    slabs, owned, width = codes_ref.shape
    per = width // LANES
    round_rows(residual_ref, rows_ref)
    fill_hankel(rows_ref, turned_rows_ref, hankel_ref)
    frames_out[...] = hankel_ref[pl.ds(me_ref[0] * per, 2 * per - 1)]
    atoms = atoms_ref[...]
    atoms_b = atoms.astype(BF16)
    cutoff = CODE_STEP * thresholds_ref[...]
    gradient_ref[...] = jnp.zeros_like(gradient_ref)
    codes_out[0] = jnp.zeros((owned, width), BF16)

    def body(n):
        frames = windows_of(hankel_ref, n, width)
        code = codes_ref[n]
        both = dot(jnp.concatenate([atoms_b, code], axis=0), frames, ((1,), (0,)))
        gradient_ref[...] += both[owned:]
        value = code.astype(F32) + (CODE_STEP * factor) * both[:owned]
        codes_out[n + 1] = soft(value, cutoff).astype(BF16)

    repeat(slabs, body)
    after = normalised(atoms + factor * gradient_ref[...])
    atoms_out[...] = after
    after_b = after.astype(BF16)
    taps = stacked_taps(after_b)
    taps_out[...] = taps
    rebuild(taps, lambda n: codes_out[n + 1], slabs, width, turned_ref, sums_ref)
    partial_residual(me_ref[0], factor, signal_ref, sums_ref, part_out)


def third_kernel(
    factor, buffers, me_ref, frames_ref, residual_ref, atoms_ref, owned_codes_ref, codes_ref, thresholds_ref, *refs
):
    before_refs, after_refs = refs[:buffers], refs[buffers : 2 * buffers]
    atoms_out, residual_out, codes_out, rows_ref, turned_rows_ref, hankel_ref, gradient_ref = refs[2 * buffers :]
    slabs, owned, width = owned_codes_ref.shape
    slabs -= 1
    per, reach = width // LANES, atoms_ref.shape[1] // LANES
    me = me_ref[0]
    round_rows(residual_ref, rows_ref)
    fill_hankel(rows_ref, turned_rows_ref, hankel_ref)
    frames = windows_of(frames_ref, 0, width), windows_of(hankel_ref, me, width)
    each = slabs // buffers
    together = max(1, min(each, 256 // owned))

    def atoms_at(ref, b):
        taps = [ref[(b * reach + p) * owned : (b * reach + p + 1) * owned, :] for p in range(reach)]
        return jnp.concatenate(taps, axis=1)

    for i in range(buffers):
        for start in range(0, each, together):
            places = range(start, start + together)
            there = [pl.ds(pl.multiple_of(owner_of(me, i * each + b, slabs) * owned, owned), owned) for b in places]
            value = jnp.concatenate([codes_ref[own, :] for own in there], axis=0).astype(F32)
            cutoff = CODE_STEP * jnp.concatenate([thresholds_ref[own, :] for own in there], axis=0)
            for ref, frame in ((before_refs[i], frames[0]), (after_refs[i], frames[1])):
                atoms_b = jnp.concatenate([atoms_at(ref, b) for b in places], axis=0)
                value = soft(value + (CODE_STEP * factor) * dot(atoms_b, frame, ((1,), (0,))), cutoff)
            value = value.astype(BF16)
            for b, own in enumerate(there):
                codes_out[own, :] = value[b * owned : (b + 1) * owned]
    gradient_ref[...] = jnp.zeros_like(gradient_ref)

    def body(n):
        gradient_ref[...] += dot(owned_codes_ref[n + 1], windows_of(hankel_ref, n, width), ((1,), (0,)))

    repeat(slabs, body)
    atoms_out[...] = normalised(atoms_ref[...] + factor * gradient_ref[...])
    residual_out[...] = residual_ref[pl.ds(me * per, per), :]


def call(kernel, outs, scratch, *args):
    vmem = pl.BlockSpec(memory_space=pltpu.VMEM)
    return pl.pallas_call(
        kernel,
        out_shape=outs,
        in_specs=[pl.BlockSpec(memory_space=pltpu.SMEM)] + [vmem] * (len(args) - 1),
        out_specs=jax.tree.map(lambda _: vmem, outs),
        scratch_shapes=scratch,
        compiler_params=pltpu.CompilerParams(vmem_limit_bytes=VMEM_BYTES),
    )(*args)


def swapped(block, distance):
    count = lax.axis_size("tm")
    return lax.ppermute(block, "tm", [(i, i ^ distance) for i in range(count)])


def gathered_and_summed(block, part):
    distance = lax.axis_size("tm") // 2
    rows = part.shape[0]
    buffers = [block]
    while distance:
        high = lax.reduce_precision(part, 8, 7)
        low = lax.reduce_precision(part - high, 8, 7)
        terms = [high.astype(BF16), low.astype(BF16)]
        if distance > 1:
            mine = jnp.concatenate(buffers + terms)
            other = swapped(mine, distance)
            end = mine.shape[0] - 2 * rows
            terms = other[end:]
            buffers = [mine[:end], other[:end]]
        else:
            terms = swapped(jnp.concatenate(terms), distance)
            buffers = buffers + [swapped(buffer, distance) for buffer in buffers]
        part = (high + low) + (terms[:rows].astype(F32) + terms[rows:].astype(F32))
        distance //= 2
    return buffers, part


def on_device(signal, codes, dictionary, thresholds):
    _, atom_count, width = codes.shape
    owned, lag_count = dictionary.shape
    slabs = lax.axis_size("tm")
    per = width // LANES
    blocks = slabs * per
    factor = (atom_count * lag_count) ** (-0.5)
    me = lax.axis_index("tm")
    at = me.astype(jnp.int32).reshape(1)
    signal_rows = signal.reshape(per, LANES)
    own_thresholds = lax.dynamic_slice(thresholds, (me * owned,), (owned,)).reshape(owned, 1)
    codes = codes[0]

    by_atom = lax.all_to_all(codes.reshape(slabs, owned, width), "tm", 0, 0, tiled=True)

    sums = [pltpu.VMEM((LANES, LANES), F32), pltpu.VMEM((blocks, 8, LANES), F32)]
    windows = [
        pltpu.VMEM((blocks + 8, LANES), F32),
        pltpu.VMEM((blocks + 8, 8, LANES), F32),
        pltpu.VMEM((blocks + per - 1, LANES, LANES), BF16),
        pltpu.VMEM((owned, lag_count), F32),
    ]
    atoms_shape = jax.ShapeDtypeStruct((owned, lag_count), F32)
    taps_shape = jax.ShapeDtypeStruct((owned * lag_count // LANES, LANES), BF16)
    part_shape = jax.ShapeDtypeStruct((blocks, LANES), F32)
    taps, part = call(
        functools.partial(first_kernel, factor), (taps_shape, part_shape), sums, at, dictionary, by_atom, signal_rows
    )
    before, first = gathered_and_summed(taps, part)
    atoms, taps, next_codes, part, frames = call(
        functools.partial(second_kernel, factor),
        (
            atoms_shape,
            taps_shape,
            jax.ShapeDtypeStruct((slabs + 1, owned, width), BF16),
            part_shape,
            jax.ShapeDtypeStruct((2 * per - 1, LANES, LANES), BF16),
        ),
        windows + sums,
        at, first, dictionary, by_atom, own_thresholds, signal_rows,
    )
    after, second = gathered_and_summed(taps, part)
    atoms, residual, codes = call(
        functools.partial(third_kernel, factor, len(after)),
        (
            atoms_shape,
            jax.ShapeDtypeStruct((per, LANES), F32),
            jax.ShapeDtypeStruct((atom_count, width), BF16),
        ),
        windows,
        at, frames, second, atoms, next_codes, codes, thresholds.reshape(atom_count, 1), *before, *after,
    )
    return codes[None], atoms, residual.reshape(1, width)


def solution(mesh):
    return jax.shard_map(
        on_device,
        mesh=mesh,
        in_specs=(P("groups", "tm"), P("groups", None, "tm"), P("tm", None), P()),
        out_specs=(P("groups", None, "tm"), P(("groups", "tm"), None), P("groups", "tm")),
        check_vma=False,
    )
```

```python
import functools
import math

import jax
import jax.numpy as jnp
from jax import lax
from jax.experimental import pallas as pl
from jax.experimental.pallas import tpu as pltpu
from jax.sharding import PartitionSpec as P

CODE_STEP = 6.0
EPSILON = 1e-06
LANES = 128
F32, BF16 = jnp.float32, jnp.bfloat16


def dot(a, b, dims):
    return lax.dot_general(a, b, (dims, ((), ())), preferred_element_type=F32)


def repeat(count, body, carry=None):
    def step(i, carry):
        return body(i) if carry is None else body(i, carry)

    if count > 80:
        return lax.fori_loop(0, count, step, carry)
    for i in range(count):
        carry = step(i, carry)
    return carry


def row_lane():
    shape = (LANES, LANES)
    return lax.broadcasted_iota(jnp.int32, shape, 0), lax.broadcasted_iota(jnp.int32, shape, 1)


def fill_hankel(rows_ref, turned_ref, hankel_ref):
    count = hankel_ref.shape[0]
    q = lax.broadcasted_iota(jnp.int32, (8, LANES), 0)
    v = lax.broadcasted_iota(jnp.int32, (8, LANES), 1)

    def turn(m):
        group = jnp.broadcast_to(rows_ref[pl.ds(m, 1), :], (8, LANES))
        for bit in (1, 2, 4):
            group = jnp.where((q & bit) != 0, pltpu.roll(group, LANES - bit, 1), group)
        turned_ref[m] = group

    repeat(count + 1, turn)
    for a in range(0, LANES, 16):
        keeps = [q + v + (a + b) < LANES for b in (0, 8)]

        def groups(m):
            group = turned_ref[m]
            return tuple(pltpu.roll(group, LANES - a - b, 1) if a + b else group for b in (0, 8))

        def place(m, here):
            after = groups(m + 1)
            pair = [jnp.where(keep, old, new) for keep, old, new in zip(keeps, here, after)]
            hankel_ref[m, a : a + 16, :] = jnp.concatenate(pair, axis=0).astype(BF16)
            return after

        repeat(count, place, groups(0))


def windows_of(hankel_ref, slab, width):
    per = width // LANES
    rows = [
        jnp.concatenate([hankel_ref[slab * per + p + i] for i in range(per)], axis=1)
        for p in range(per)
    ]
    return jnp.concatenate(rows, axis=0)


def soft(value, cutoff):
    return value - jnp.minimum(jnp.maximum(value, -cutoff), cutoff)


def normalised(updated):
    return updated / jnp.sqrt(jnp.mean(updated * updated, axis=1, keepdims=True) + EPSILON)


def stacked_taps(atoms):
    return jnp.concatenate([atoms[:, i : i + LANES] for i in range(0, atoms.shape[1], LANES)], axis=0)


def rebuild(taps, slab_of, slabs, width, turned_ref, sums_ref):
    per = width // LANES
    q, v = row_lane()
    keep = v >= q
    turned_ref[...] = jnp.zeros_like(turned_ref)

    def body(n):
        now, before = slab_of(n), slab_of(n - 1)
        shifted = [now] + [
            jnp.concatenate([before[:, width - LANES * p :], now[:, : width - LANES * p]], axis=1) for p in range(1, per)
        ]
        products = dot(taps, jnp.concatenate(shifted, axis=0), ((0,), (0,)))
        last = turned_ref[...]
        for i in range(per):
            turned = pltpu.roll(products[:, LANES * i : LANES * (i + 1)], 0, 1, stride=1, stride_axis=0)
            placed = jnp.where(keep, turned, last)
            sums_ref[n * per + i] = placed.reshape(LANES // 8, 8, LANES).sum(axis=0)
            last = turned
        turned_ref[...] = last

    repeat(slabs, body)


def partial_residual(me, factor, signal_ref, sums_ref, out_ref):
    rows = signal_ref.shape[0]
    out_ref[...] = -factor * jnp.sum(sums_ref[...], axis=1)
    own = pl.ds(me * rows, rows)
    out_ref[own, :] = out_ref[own, :] + signal_ref[...]


def owner_of(me, place, count):
    distance, bit = count // 2, 0
    while distance:
        if place >> bit & 1:
            me = me ^ distance
        distance, bit = distance // 2, bit + 1
    return me


def first_kernel(factor, me_ref, atoms_ref, codes_ref, signal_ref, taps_out, part_out, turned_ref, sums_ref):
    slabs, owned, width = codes_ref.shape
    taps = stacked_taps(atoms_ref[...].astype(BF16))
    taps_out[...] = taps
    zero = jnp.zeros((owned, width), BF16)

    def slab_of(n):
        if isinstance(n, int):
            return codes_ref[n] if n >= 0 else zero
        return jnp.where(n >= 0, codes_ref[jnp.maximum(n, 0)], zero)

    rebuild(taps, slab_of, slabs, width, turned_ref, sums_ref)
    partial_residual(me_ref[0], factor, signal_ref, sums_ref, part_out)


def round_rows(residual_ref, rows_ref):
    count = residual_ref.shape[0]
    rows_ref[:count, :] = residual_ref[...].astype(BF16).astype(F32)
    rows_ref[count:, :] = jnp.zeros((rows_ref.shape[0] - count, LANES), F32)


def second_kernel(
    factor, me_ref, residual_ref, atoms_ref, codes_ref, thresholds_ref, signal_ref,
    atoms_out, taps_out, codes_out, part_out, frames_out,
    rows_ref, turned_rows_ref, hankel_ref, gradient_ref, turned_ref, sums_ref,
):
    slabs, owned, width = codes_ref.shape
    per = width // LANES
    round_rows(residual_ref, rows_ref)
    fill_hankel(rows_ref, turned_rows_ref, hankel_ref)
    frames_out[...] = hankel_ref[pl.ds(me_ref[0] * per, 2 * per - 1)]
    atoms = atoms_ref[...]
    atoms_b = atoms.astype(BF16)
    cutoff = CODE_STEP * thresholds_ref[...]
    gradient_ref[...] = jnp.zeros_like(gradient_ref)
    codes_out[0] = jnp.zeros((owned, width), BF16)

    def body(n):
        frames = windows_of(hankel_ref, n, width)
        code = codes_ref[n]
        both = dot(jnp.concatenate([atoms_b, code], axis=0), frames, ((1,), (0,)))
        gradient_ref[...] += both[owned:]
        value = code.astype(F32) + (CODE_STEP * factor) * both[:owned]
        codes_out[n + 1] = soft(value, cutoff).astype(BF16)

    repeat(slabs, body)
    after = normalised(atoms + factor * gradient_ref[...])
    atoms_out[...] = after
    after_b = after.astype(BF16)
    taps = stacked_taps(after_b)
    taps_out[...] = taps
    rebuild(taps, lambda n: codes_out[n + 1], slabs, width, turned_ref, sums_ref)
    partial_residual(me_ref[0], factor, signal_ref, sums_ref, part_out)


def atoms_at(ref, places, owned, reach):
    taps = [[ref[(b * reach + p) * owned : (b * reach + p + 1) * owned, :] for p in range(reach)] for b in places]
    return jnp.concatenate([jnp.concatenate(row, axis=1) for row in taps], axis=0)


def rows_at(me, first, places, owned, count):
    return [pl.ds(pl.multiple_of(owner_of(me, first + b, count) * owned, owned), owned) for b in places]


def batches(each, owned):
    together = max(1, min(each, 256 // owned))
    return [range(start, start + together) for start in range(0, each, together)]


def shrink_kernel(factor, count, owned, me_ref, frames_ref, codes_ref, thresholds_ref, *refs):
    buffers, values_out = refs[:-1], refs[-1]
    width = codes_ref.shape[1]
    reach = width // LANES
    frames = windows_of(frames_ref, 0, width)
    each = count // len(buffers)
    for i, ref in enumerate(buffers):
        for places in batches(each, owned):
            there = rows_at(me_ref[0], i * each, places, owned, count)
            value = jnp.concatenate([codes_ref[own, :] for own in there], axis=0).astype(F32)
            cutoff = CODE_STEP * jnp.concatenate([thresholds_ref[own, :] for own in there], axis=0)
            value += (CODE_STEP * factor) * dot(atoms_at(ref, places, owned, reach), frames, ((1,), (0,)))
            first = (i * each + places[0]) * owned
            values_out[first : first + value.shape[0], :] = soft(value, cutoff)


def third_kernel(
    factor, me_ref, residual_ref, atoms_ref, owned_codes_ref, values_ref, thresholds_ref, *refs
):
    buffers = refs[:-7]
    atoms_out, residual_out, codes_out, rows_ref, turned_rows_ref, hankel_ref, gradient_ref = refs[-7:]
    slabs, owned, width = owned_codes_ref.shape
    slabs -= 1
    per, reach = width // LANES, atoms_ref.shape[1] // LANES
    me = me_ref[0]
    round_rows(residual_ref, rows_ref)
    fill_hankel(rows_ref, turned_rows_ref, hankel_ref)
    frames = windows_of(hankel_ref, me, width)
    each = slabs // len(buffers)
    for i, ref in enumerate(buffers):
        for places in batches(each, owned):
            there = rows_at(me, i * each, places, owned, slabs)
            cutoff = CODE_STEP * jnp.concatenate([thresholds_ref[own, :] for own in there], axis=0)
            first = (i * each + places[0]) * owned
            change = (CODE_STEP * factor) * dot(atoms_at(ref, places, owned, reach), frames, ((1,), (0,)))
            value = soft(values_ref[first : first + change.shape[0], :] + change, cutoff).astype(BF16)
            for b, own in enumerate(there):
                codes_out[own, :] = value[b * owned : (b + 1) * owned]
    gradient_ref[...] = jnp.zeros_like(gradient_ref)

    def body(n):
        gradient_ref[...] += dot(owned_codes_ref[n + 1], windows_of(hankel_ref, n, width), ((1,), (0,)))

    repeat(slabs, body)
    atoms_out[...] = normalised(atoms_ref[...] + factor * gradient_ref[...])
    residual_out[...] = residual_ref[pl.ds(me * per, per), :]


def call(kernel, outs, scratch, *args):
    held = [(a.shape, a.dtype) for a in [*args[1:], *jax.tree.leaves(outs)]] + [(a.shape, a.dtype) for a in scratch]
    room = sum(math.prod(shape) * jnp.dtype(kind).itemsize for shape, kind in held)
    vmem = pl.BlockSpec(memory_space=pltpu.VMEM)
    return pl.pallas_call(
        kernel,
        out_shape=outs,
        in_specs=[pl.BlockSpec(memory_space=pltpu.SMEM)] + [vmem] * (len(args) - 1),
        out_specs=jax.tree.map(lambda _: vmem, outs),
        scratch_shapes=scratch,
        compiler_params=pltpu.CompilerParams(vmem_limit_bytes=room + 6 * 1024 * 1024),
    )(*args)


def swapped(block, distance):
    count = lax.axis_size("tm")
    return lax.ppermute(block, "tm", [(i, i ^ distance) for i in range(count)])


def tied(value, *others):
    return lax.optimization_barrier((value, others))[0]


def exchanged(block, part, alone, late=None):
    distance = lax.axis_size("tm") // 2
    rows = part.shape[0]
    buffers = [block]
    while distance:
        high = lax.reduce_precision(part, 8, 7)
        low = lax.reduce_precision(part - high, 8, 7)
        sent = [high.astype(BF16), low.astype(BF16)]
        if distance > alone:
            sent = buffers + sent
        sent = jnp.concatenate(sent)
        if distance == 2 and late is not None:
            sent = tied(sent, late)
        other = swapped(sent, distance)
        end = sent.shape[0] - 2 * rows
        if distance > alone:
            buffers = [sent[:end], other[:end]]
        part = (high + low) + (other[end : end + rows].astype(F32) + other[end + rows :].astype(F32))
        distance //= 2
    return buffers, part


def on_device(signal, codes, dictionary, thresholds):
    _, atom_count, width = codes.shape
    owned, lag_count = dictionary.shape
    slabs = lax.axis_size("tm")
    per = width // LANES
    blocks = slabs * per
    factor = (atom_count * lag_count) ** (-0.5)
    me = lax.axis_index("tm")
    at = me.astype(jnp.int32).reshape(1)
    signal_rows = signal.reshape(per, LANES)
    own_thresholds = lax.dynamic_slice(thresholds, (me * owned,), (owned,)).reshape(owned, 1)
    codes = codes[0]

    by_atom = lax.all_to_all(codes.reshape(slabs, owned, width), "tm", 0, 0, tiled=True)

    sums = [pltpu.VMEM((LANES, LANES), F32), pltpu.VMEM((blocks, 8, LANES), F32)]
    windows = [
        pltpu.VMEM((blocks + 8, LANES), F32),
        pltpu.VMEM((blocks + 8, 8, LANES), F32),
        pltpu.VMEM((blocks + per - 1, LANES, LANES), BF16),
        pltpu.VMEM((owned, lag_count), F32),
    ]
    atoms_shape = jax.ShapeDtypeStruct((owned, lag_count), F32)
    taps_shape = jax.ShapeDtypeStruct((owned * lag_count // LANES, LANES), BF16)
    part_shape = jax.ShapeDtypeStruct((blocks, LANES), F32)
    taps, part = call(
        functools.partial(first_kernel, factor), (taps_shape, part_shape), sums, at, dictionary, by_atom, signal_rows
    )
    before, first = exchanged(taps, part, 2)
    atoms, taps, next_codes, part, frames = call(
        functools.partial(second_kernel, factor),
        (
            atoms_shape,
            taps_shape,
            jax.ShapeDtypeStruct((slabs + 1, owned, width), BF16),
            part_shape,
            jax.ShapeDtypeStruct((2 * per - 1, LANES, LANES), BF16),
        ),
        windows + sums,
        at, first, dictionary, by_atom, own_thresholds, signal_rows,
    )
    all_thresholds = thresholds.reshape(atom_count, 1)
    mine = jnp.concatenate(before)
    other = swapped(tied(mine, part), 2)
    before = [mine, other, swapped(mine, 1), swapped(other, 1)]
    after, second = exchanged(taps, part, 1, other)
    after = after + [swapped(buffer, 1) for buffer in after]
    values = call(
        functools.partial(shrink_kernel, factor, slabs, owned),
        jax.ShapeDtypeStruct((atom_count, width), F32),
        [],
        at, frames, codes, all_thresholds, *before,
    )
    atoms, residual, codes = call(
        functools.partial(third_kernel, factor),
        (
            atoms_shape,
            jax.ShapeDtypeStruct((per, LANES), F32),
            jax.ShapeDtypeStruct((atom_count, width), BF16),
        ),
        windows,
        at, second, atoms, next_codes, values, all_thresholds, *after,
    )
    return codes[None], atoms, residual.reshape(1, width)


def solution(mesh):
    return jax.shard_map(
        on_device,
        mesh=mesh,
        in_specs=(P("groups", "tm"), P("groups", None, "tm"), P("tm", None), P()),
        out_specs=(P("groups", None, "tm"), P(("groups", "tm"), None), P("groups", "tm")),
        check_vma=False,
    )
```

```python
import functools
import math

import jax
import jax.numpy as jnp
from jax import lax
from jax.experimental import pallas as pl
from jax.experimental.pallas import tpu as pltpu
from jax.sharding import PartitionSpec as P

CODE_STEP = 6.0
EPSILON = 1e-06
LANES = 128
F32, BF16 = jnp.float32, jnp.bfloat16


def dot(a, b, dims):
    return lax.dot_general(a, b, (dims, ((), ())), preferred_element_type=F32)


def repeat(count, body, carry=None):
    def step(i, carry):
        return body(i) if carry is None else body(i, carry)

    if count > 80:
        return lax.fori_loop(0, count, step, carry)
    for i in range(count):
        carry = step(i, carry)
    return carry


def row_lane():
    shape = (LANES, LANES)
    return lax.broadcasted_iota(jnp.int32, shape, 0), lax.broadcasted_iota(jnp.int32, shape, 1)


def fill_hankel(rows_ref, turned_ref, hankel_ref):
    count = hankel_ref.shape[0]
    q = lax.broadcasted_iota(jnp.int32, (8, LANES), 0)
    v = lax.broadcasted_iota(jnp.int32, (8, LANES), 1)

    def turn(m):
        group = jnp.broadcast_to(rows_ref[pl.ds(m, 1), :], (8, LANES))
        for bit in (1, 2, 4):
            group = jnp.where((q & bit) != 0, pltpu.roll(group, LANES - bit, 1), group)
        turned_ref[m] = group

    repeat(count + 1, turn)
    for a in range(0, LANES, 16):
        keeps = [q + v + (a + b) < LANES for b in (0, 8)]

        def groups(m):
            group = turned_ref[m]
            return tuple(pltpu.roll(group, LANES - a - b, 1) if a + b else group for b in (0, 8))

        def place(m, here):
            after = groups(m + 1)
            pair = [jnp.where(keep, old, new) for keep, old, new in zip(keeps, here, after)]
            hankel_ref[m, a : a + 16, :] = jnp.concatenate(pair, axis=0).astype(BF16)
            return after

        repeat(count, place, groups(0))


def windows_of(hankel_ref, slab, width):
    per = width // LANES
    rows = [
        jnp.concatenate([hankel_ref[slab * per + p + i] for i in range(per)], axis=1)
        for p in range(per)
    ]
    return jnp.concatenate(rows, axis=0)


def soft(value, cutoff):
    return value - jnp.minimum(jnp.maximum(value, -cutoff), cutoff)


def normalised(updated):
    return updated / jnp.sqrt(jnp.mean(updated * updated, axis=1, keepdims=True) + EPSILON)


def stacked_taps(atoms):
    return jnp.concatenate([atoms[:, i : i + LANES] for i in range(0, atoms.shape[1], LANES)], axis=0)


def rebuild(taps, slab_of, slabs, width, turned_ref, sums_ref):
    per = width // LANES
    q, v = row_lane()
    keep = v >= q
    turned_ref[...] = jnp.zeros_like(turned_ref)

    def body(n):
        now, before = slab_of(n), slab_of(n - 1)
        shifted = [now] + [
            jnp.concatenate([before[:, width - LANES * p :], now[:, : width - LANES * p]], axis=1) for p in range(1, per)
        ]
        products = dot(taps, jnp.concatenate(shifted, axis=0), ((0,), (0,)))
        last = turned_ref[...]
        for i in range(per):
            turned = pltpu.roll(products[:, LANES * i : LANES * (i + 1)], 0, 1, stride=1, stride_axis=0)
            placed = jnp.where(keep, turned, last)
            sums_ref[n * per + i] = placed.reshape(LANES // 8, 8, LANES).sum(axis=0)
            last = turned
        turned_ref[...] = last

    repeat(slabs, body)


def partial_residual(me, factor, signal_ref, sums_ref, out_ref):
    rows = signal_ref.shape[0]
    out_ref[...] = -factor * jnp.sum(sums_ref[...], axis=1)
    own = pl.ds(me * rows, rows)
    out_ref[own, :] = out_ref[own, :] + signal_ref[...]


def owner_of(me, place, count):
    distance, bit = count // 2, 0
    while distance:
        if place >> bit & 1:
            me = me ^ distance
        distance, bit = distance // 2, bit + 1
    return me


def first_kernel(factor, me_ref, atoms_ref, codes_ref, signal_ref, taps_out, part_out, turned_ref, sums_ref):
    slabs, owned, width = codes_ref.shape
    taps = stacked_taps(atoms_ref[...].astype(BF16))
    taps_out[...] = taps
    zero = jnp.zeros((owned, width), BF16)

    def slab_of(n):
        if isinstance(n, int):
            return codes_ref[n] if n >= 0 else zero
        return jnp.where(n >= 0, codes_ref[jnp.maximum(n, 0)], zero)

    rebuild(taps, slab_of, slabs, width, turned_ref, sums_ref)
    partial_residual(me_ref[0], factor, signal_ref, sums_ref, part_out)


def whole_residual(terms):
    rows = terms[0].shape[0] // 2
    mine, other = (ref[:rows, :].astype(F32) + ref[rows:, :].astype(F32) for ref in terms)
    return mine + other


def round_rows(residual, rows_ref):
    count = residual.shape[0]
    rows_ref[:count, :] = residual.astype(BF16).astype(F32)
    rows_ref[count:, :] = jnp.zeros((rows_ref.shape[0] - count, LANES), F32)


def kept_at(piece, slabs, per):
    lane = piece % per * LANES
    return slabs + 3 + piece // per, slice(lane, lane + LANES)


def second_kernel(
    factor, me_ref, sent_ref, other_ref, atoms_ref, codes_ref, thresholds_ref, signal_ref,
    taps_out, codes_out, part_out,
    rows_ref, turned_rows_ref, hankel_ref, gradient_ref, turned_ref, sums_ref,
):
    slabs, owned, width = codes_ref.shape
    per = width // LANES
    round_rows(whole_residual((sent_ref, other_ref)), rows_ref)
    fill_hankel(rows_ref, turned_rows_ref, hankel_ref)
    for m in range(2 * per - 1):
        block = hankel_ref[me_ref[0] * per + m]
        for h in range(LANES // owned):
            slab, lane = kept_at(m * (LANES // owned) + h, slabs, per)
            codes_out[slab, :, lane] = block[h * owned : (h + 1) * owned, :]
    atoms = atoms_ref[...]
    atoms_b = atoms.astype(BF16)
    cutoff = CODE_STEP * thresholds_ref[...]
    gradient_ref[...] = jnp.zeros_like(gradient_ref)
    codes_out[0] = jnp.zeros((owned, width), BF16)

    def body(n):
        frames = windows_of(hankel_ref, n, width)
        code = codes_ref[n]
        both = dot(jnp.concatenate([atoms_b, code], axis=0), frames, ((1,), (0,)))
        gradient_ref[...] += both[owned:]
        value = code.astype(F32) + (CODE_STEP * factor) * both[:owned]
        codes_out[n + 1] = soft(value, cutoff).astype(BF16)

    repeat(slabs, body)
    after = normalised(atoms + factor * gradient_ref[...])
    after_b = after.astype(BF16)
    codes_out[slabs + 1] = after_b
    codes_out[slabs + 2] = (after - after_b.astype(F32)).astype(BF16)
    taps = stacked_taps(after_b)
    taps_out[...] = taps
    rebuild(taps, lambda n: codes_out[n + 1], slabs, width, turned_ref, sums_ref)
    partial_residual(me_ref[0], factor, signal_ref, sums_ref, part_out)


def atoms_at(ref, places, owned, reach):
    taps = [[ref[(b * reach + p) * owned : (b * reach + p + 1) * owned, :] for p in range(reach)] for b in places]
    return jnp.concatenate([jnp.concatenate(row, axis=1) for row in taps], axis=0)


def rows_at(me, first, places, owned, count):
    return [pl.ds(pl.multiple_of(owner_of(me, first + b, count) * owned, owned), owned) for b in places]


def batches(each, owned):
    together = max(1, min(each, 256 // owned))
    return [range(start, start + together) for start in range(0, each, together)]


def third_kernel(
    factor, buffers, me_ref, sent_ref, other_ref, kept_ref, codes_ref, thresholds_ref, *refs
):
    before_refs, after_refs = refs[:buffers], refs[buffers : 2 * buffers]
    atoms_out, residual_out, codes_out = refs[2 * buffers : 2 * buffers + 3]
    rows_ref, turned_rows_ref, hankel_ref, gradient_ref = refs[2 * buffers + 3 :]
    owned, lag_count = atoms_out.shape
    atom_count, width = codes_ref.shape
    slabs, per, reach = atom_count // owned, width // LANES, lag_count // LANES
    me = me_ref[0]
    residual = whole_residual((sent_ref, other_ref))
    round_rows(residual, rows_ref)
    fill_hankel(rows_ref, turned_rows_ref, hankel_ref)
    pieces = [kept_at(piece, slabs, per) for piece in range((2 * per - 1) * (LANES // owned))]
    pieces = [kept_ref[slab, :, lane] for slab, lane in pieces]
    blocks = [jnp.concatenate(pieces[i : i + LANES // owned], axis=0) for i in range(0, len(pieces), LANES // owned)]
    frames = windows_of(blocks, 0, width), windows_of(hankel_ref, me, width)
    each = slabs // buffers
    for i in range(buffers):
        for places in batches(each, owned):
            there = rows_at(me, i * each, places, owned, slabs)
            cutoff = CODE_STEP * jnp.concatenate([thresholds_ref[own, :] for own in there], axis=0)
            value = jnp.concatenate([codes_ref[own, :] for own in there], axis=0).astype(F32)
            for ref, frame in ((before_refs[i], frames[0]), (after_refs[i], frames[1])):
                change = dot(atoms_at(ref, places, owned, reach), frame, ((1,), (0,)))
                value = soft(value + (CODE_STEP * factor) * change, cutoff)
            value = value.astype(BF16)
            for b, own in enumerate(there):
                codes_out[own, :] = value[b * owned : (b + 1) * owned]
    gradient_ref[...] = jnp.zeros_like(gradient_ref)

    def body(n):
        gradient_ref[...] += dot(kept_ref[n + 1], windows_of(hankel_ref, n, width), ((1,), (0,)))

    repeat(slabs, body)
    atoms = kept_ref[slabs + 1].astype(F32) + kept_ref[slabs + 2].astype(F32)
    atoms_out[...] = normalised(atoms + factor * gradient_ref[...])
    rows_ref[: slabs * per, :] = residual
    residual_out[...] = rows_ref[pl.ds(me * per, per), :]


def call(kernel, outs, scratch, *args):
    vmem = pl.BlockSpec(memory_space=pltpu.VMEM)
    room = sum(math.prod(a.shape) * jnp.dtype(a.dtype).itemsize for a in [*args, *outs, *scratch])
    return pl.pallas_call(
        kernel,
        out_shape=tuple(outs),
        in_specs=[pl.BlockSpec(memory_space=pltpu.SMEM)] + [vmem] * (len(args) - 1),
        out_specs=(vmem,) * len(outs),
        scratch_shapes=scratch,
        compiler_params=pltpu.CompilerParams(vmem_limit_bytes=room + 6 * 1024 * 1024),
    )(*args)


def swapped(block, distance):
    count = lax.axis_size("tm")
    return lax.ppermute(block, "tm", [(i, i ^ distance) for i in range(count)])


def tied(value, *others):
    return lax.optimization_barrier((value, others))[0]


def exchanged(block, part, alone, late={}):
    distance = lax.axis_size("tm") // 2
    rows = part.shape[0]
    buffers = [block]
    while True:
        high = lax.reduce_precision(part, 8, 7)
        low = lax.reduce_precision(part - high, 8, 7)
        sent = [high.astype(BF16), low.astype(BF16)]
        if distance > alone:
            sent = buffers + sent
        sent = jnp.concatenate(sent)
        if distance in late:
            sent = tied(sent, late[distance])
        other = swapped(sent, distance)
        end = sent.shape[0] - 2 * rows
        if distance > alone:
            buffers = [sent[:end], other[:end]]
            whole = [sent, other]
        if distance == 1:
            return buffers, whole, (sent, other)
        part = (high + low) + (other[end : end + rows].astype(F32) + other[end + rows :].astype(F32))
        distance //= 2


def on_device(signal, codes, dictionary, thresholds):
    _, atom_count, width = codes.shape
    owned, lag_count = dictionary.shape
    slabs = lax.axis_size("tm")
    per = width // LANES
    blocks = slabs * per
    factor = (atom_count * lag_count) ** (-0.5)
    me = lax.axis_index("tm")
    at = me.astype(jnp.int32).reshape(1)
    signal_rows = signal.reshape(per, LANES)
    own_thresholds = lax.dynamic_slice(thresholds, (me * owned,), (owned,)).reshape(owned, 1)
    codes = codes[0]

    by_atom = lax.all_to_all(codes.reshape(slabs, owned, width), "tm", 0, 0, tiled=True)

    sums = [pltpu.VMEM((LANES, LANES), F32), pltpu.VMEM((blocks, 8, LANES), F32)]
    windows = [
        pltpu.VMEM((blocks + 8, LANES), F32),
        pltpu.VMEM((blocks + 8, 8, LANES), F32),
        pltpu.VMEM((blocks + per - 1, LANES, LANES), BF16),
        pltpu.VMEM((owned, lag_count), F32),
    ]
    atoms_shape = jax.ShapeDtypeStruct((owned, lag_count), F32)
    taps_shape = jax.ShapeDtypeStruct((owned * lag_count // LANES, LANES), BF16)
    part_shape = jax.ShapeDtypeStruct((blocks, LANES), F32)
    taps, part = call(
        functools.partial(first_kernel, factor), (taps_shape, part_shape), sums, at, dictionary, by_atom, signal_rows
    )
    before, _, first = exchanged(taps, part, 2)
    kept = slabs + 3 + pl.cdiv((2 * per - 1) * (LANES // owned), per)
    taps, kept, part = call(
        functools.partial(second_kernel, factor),
        [taps_shape, jax.ShapeDtypeStruct((kept, owned, width), BF16), part_shape],
        windows + sums,
        at, *first, dictionary, by_atom, own_thresholds, signal_rows,
    )
    all_thresholds = thresholds.reshape(atom_count, 1)
    mine = jnp.concatenate(before)
    other = swapped(tied(mine, part), 2)
    before = [mine, other, swapped(mine, 1), swapped(other, 1)]
    _, after, second = exchanged(taps, part, 1, {4: other})
    after = after + [swapped(buffer, 1) for buffer in after]
    atoms, residual, codes = call(
        functools.partial(third_kernel, factor, len(after)),
        [
            atoms_shape,
            jax.ShapeDtypeStruct((per, LANES), F32),
            jax.ShapeDtypeStruct((atom_count, width), BF16),
        ],
        windows,
        at, *second, kept, codes, all_thresholds, *before, *after,
    )
    return codes[None], atoms, residual.reshape(1, width)


def solution(mesh):
    return jax.shard_map(
        on_device,
        mesh=mesh,
        in_specs=(P("groups", "tm"), P("groups", None, "tm"), P("tm", None), P()),
        out_specs=(P("groups", None, "tm"), P(("groups", "tm"), None), P("groups", "tm")),
        check_vma=False,
    )
```

```python
import functools
import math

import jax
import jax.numpy as jnp
from jax import lax
from jax.experimental import pallas as pl
from jax.experimental.pallas import tpu as pltpu
from jax.sharding import PartitionSpec as P

CODE_STEP = 6.0
EPSILON = 1e-06
LANES = 128
F32, BF16 = jnp.float32, jnp.bfloat16


def dot(a, b, dims):
    return lax.dot_general(a, b, (dims, ((), ())), preferred_element_type=F32)


def repeat(count, body, carry=None):
    def step(i, carry):
        return body(i) if carry is None else body(i, carry)

    if count > 80:
        return lax.fori_loop(0, count, step, carry)
    for i in range(count):
        carry = step(i, carry)
    return carry


def row_lane():
    shape = (LANES, LANES)
    return lax.broadcasted_iota(jnp.int32, shape, 0), lax.broadcasted_iota(jnp.int32, shape, 1)


def fill_hankel(rows_ref, turned_ref, hankel_ref):
    count = hankel_ref.shape[0]
    q = lax.broadcasted_iota(jnp.int32, (8, LANES), 0)
    v = lax.broadcasted_iota(jnp.int32, (8, LANES), 1)

    def turn(m):
        group = jnp.broadcast_to(rows_ref[pl.ds(m, 1), :], (8, LANES))
        for bit in (1, 2, 4):
            group = jnp.where((q & bit) != 0, pltpu.roll(group, LANES - bit, 1), group)
        turned_ref[m] = group

    repeat(count + 1, turn)
    for a in range(0, LANES, 16):
        keeps = [q + v + (a + b) < LANES for b in (0, 8)]

        def groups(m):
            group = turned_ref[m]
            return tuple(pltpu.roll(group, LANES - a - b, 1) if a + b else group for b in (0, 8))

        def place(m, here):
            after = groups(m + 1)
            pair = [jnp.where(keep, old, new) for keep, old, new in zip(keeps, here, after)]
            hankel_ref[m, a : a + 16, :] = jnp.concatenate(pair, axis=0).astype(BF16)
            return after

        repeat(count, place, groups(0))


def windows_of(hankel_ref, slab, width):
    per = width // LANES
    rows = [
        jnp.concatenate([hankel_ref[slab * per + p + i] for i in range(per)], axis=1)
        for p in range(per)
    ]
    return jnp.concatenate(rows, axis=0)


def soft(value, cutoff):
    return value - jnp.minimum(jnp.maximum(value, -cutoff), cutoff)


def normalised(updated):
    return updated / jnp.sqrt(jnp.mean(updated * updated, axis=1, keepdims=True) + EPSILON)


def stacked_taps(atoms):
    return jnp.concatenate([atoms[:, i : i + LANES] for i in range(0, atoms.shape[1], LANES)], axis=0)


def rebuild(taps, slab_of, slabs, width, turned_ref, sums_ref):
    per = width // LANES
    q, v = row_lane()
    keep = v >= q
    turned_ref[...] = jnp.zeros_like(turned_ref)

    def body(n):
        now, before = slab_of(n), slab_of(n - 1)
        shifted = [now] + [
            jnp.concatenate([before[:, width - LANES * p :], now[:, : width - LANES * p]], axis=1) for p in range(1, per)
        ]
        products = dot(taps, jnp.concatenate(shifted, axis=0), ((0,), (0,)))
        last = turned_ref[...]
        for i in range(per):
            turned = pltpu.roll(products[:, LANES * i : LANES * (i + 1)], 0, 1, stride=1, stride_axis=0)
            placed = jnp.where(keep, turned, last)
            sums_ref[n * per + i] = placed.reshape(LANES // 8, 8, LANES).sum(axis=0)
            last = turned
        turned_ref[...] = last

    repeat(slabs, body)


def partial_residual(me, factor, signal_ref, sums_ref, out_ref):
    rows = signal_ref.shape[0]
    out_ref[...] = -factor * jnp.sum(sums_ref[...], axis=1)
    own = pl.ds(me * rows, rows)
    out_ref[own, :] = out_ref[own, :] + signal_ref[...]


def owner_of(me, place, count):
    distance, bit = count // 2, 0
    while distance:
        if place >> bit & 1:
            me = me ^ distance
        distance, bit = distance // 2, bit + 1
    return me


def first_kernel(factor, me_ref, atoms_ref, codes_ref, signal_ref, taps_out, part_out, turned_ref, sums_ref):
    slabs, owned, width = codes_ref.shape
    taps = stacked_taps(atoms_ref[...].astype(BF16))
    taps_out[...] = taps
    zero = jnp.zeros((owned, width), BF16)

    def slab_of(n):
        if isinstance(n, int):
            return codes_ref[n] if n >= 0 else zero
        return jnp.where(n >= 0, codes_ref[jnp.maximum(n, 0)], zero)

    rebuild(taps, slab_of, slabs, width, turned_ref, sums_ref)
    partial_residual(me_ref[0], factor, signal_ref, sums_ref, part_out)


def whole_residual(terms):
    rows = terms[0].shape[0] // 2
    mine, other = (ref[:rows, :].astype(F32) + ref[rows:, :].astype(F32) for ref in terms)
    return mine + other


def round_rows(residual, rows_ref):
    count = residual.shape[0]
    rows_ref[:count, :] = residual.astype(BF16).astype(F32)
    rows_ref[count:, :] = jnp.zeros((rows_ref.shape[0] - count, LANES), F32)


def kept_at(piece, slabs, per):
    lane = piece % per * LANES
    return slabs + 3 + piece // per, slice(lane, lane + LANES)


def second_kernel(
    factor, me_ref, sent_ref, other_ref, atoms_ref, codes_ref, thresholds_ref, signal_ref,
    taps_out, codes_out, part_out,
    rows_ref, turned_rows_ref, hankel_ref, gradient_ref, turned_ref, sums_ref,
):
    slabs, owned, width = codes_ref.shape
    per = width // LANES
    round_rows(whole_residual((sent_ref, other_ref)), rows_ref)
    fill_hankel(rows_ref, turned_rows_ref, hankel_ref)
    for m in range(2 * per - 1):
        block = hankel_ref[me_ref[0] * per + m]
        for h in range(LANES // owned):
            slab, lane = kept_at(m * (LANES // owned) + h, slabs, per)
            codes_out[slab, :, lane] = block[h * owned : (h + 1) * owned, :]
    atoms = atoms_ref[...]
    atoms_b = atoms.astype(BF16)
    cutoff = CODE_STEP * thresholds_ref[...]
    gradient_ref[...] = jnp.zeros_like(gradient_ref)
    codes_out[0] = jnp.zeros((owned, width), BF16)

    def body(n):
        frames = windows_of(hankel_ref, n, width)
        code = codes_ref[n]
        both = dot(jnp.concatenate([atoms_b, code], axis=0), frames, ((1,), (0,)))
        gradient_ref[...] += both[owned:]
        value = code.astype(F32) + (CODE_STEP * factor) * both[:owned]
        codes_out[n + 1] = soft(value, cutoff).astype(BF16)

    repeat(slabs, body)
    after = normalised(atoms + factor * gradient_ref[...])
    after_b = after.astype(BF16)
    codes_out[slabs + 1] = after_b
    codes_out[slabs + 2] = (after - after_b.astype(F32)).astype(BF16)
    taps = stacked_taps(after_b)
    taps_out[...] = taps
    rebuild(taps, lambda n: codes_out[n + 1], slabs, width, turned_ref, sums_ref)
    partial_residual(me_ref[0], factor, signal_ref, sums_ref, part_out)


def atoms_at(ref, places, owned, reach):
    taps = [[ref[(b * reach + p) * owned : (b * reach + p + 1) * owned, :] for p in range(reach)] for b in places]
    return jnp.concatenate([jnp.concatenate(row, axis=1) for row in taps], axis=0)


def rows_at(me, first, places, owned, count):
    return [pl.ds(pl.multiple_of(owner_of(me, first + b, count) * owned, owned), owned) for b in places]


def batches(each, owned):
    together = max(1, min(each, 256 // owned))
    return [range(start, start + together) for start in range(0, each, together)]


def spread(thresholds_ref, cutoffs_ref):
    count = thresholds_ref.shape[0]
    filled = jnp.concatenate([thresholds_ref[...], jnp.zeros((LANES - count, LANES), F32)], axis=0)
    columns = CODE_STEP * filled.T
    for m in range(count):
        cutoffs_ref[m * LANES : (m + 1) * LANES, :] = columns[:, m : m + 1]


def shrink_kernel(factor, owned, me_ref, kept_ref, codes_ref, thresholds_ref, *refs):
    buffers, values_out, cutoffs_ref = refs[:-2], refs[-2], refs[-1]
    atom_count, width = codes_ref.shape
    slabs, per, reach = atom_count // owned, width // LANES, width // LANES
    spread(thresholds_ref, cutoffs_ref)
    each = LANES // owned
    pieces = [kept_at(piece, slabs, per) for piece in range((2 * per - 1) * each)]
    pieces = [kept_ref[slab, :, lane] for slab, lane in pieces]
    frames = windows_of([jnp.concatenate(pieces[i : i + each], axis=0) for i in range(0, len(pieces), each)], 0, width)
    each = slabs // len(buffers)
    for i, ref in enumerate(buffers):
        for places in batches(each, owned):
            there = rows_at(me_ref[0], i * each, places, owned, slabs)
            value = jnp.concatenate([codes_ref[own, :] for own in there], axis=0).astype(F32)
            cutoff = jnp.concatenate([cutoffs_ref[own, :] for own in there], axis=0)
            value += (CODE_STEP * factor) * dot(atoms_at(ref, places, owned, reach), frames, ((1,), (0,)))
            first = (i * each + places[0]) * owned
            values_out[first : first + value.shape[0], :] = soft(value, cutoff).astype(values_out.dtype)


def third_kernel(factor, me_ref, sent_ref, other_ref, kept_ref, values_ref, thresholds_ref, *refs):
    buffers = refs[:-8]
    atoms_out, residual_out, codes_out, rows_ref, turned_rows_ref, hankel_ref, gradient_ref, cutoffs_ref = refs[-8:]
    owned, lag_count = atoms_out.shape
    atom_count, width = values_ref.shape
    slabs, per, reach = atom_count // owned, width // LANES, lag_count // LANES
    me = me_ref[0]
    residual = whole_residual((sent_ref, other_ref))
    round_rows(residual, rows_ref)
    fill_hankel(rows_ref, turned_rows_ref, hankel_ref)
    spread(thresholds_ref, cutoffs_ref)
    frames = windows_of(hankel_ref, me, width)
    each = slabs // len(buffers)
    for i, ref in enumerate(buffers):
        for places in batches(each, owned):
            there = rows_at(me, i * each, places, owned, slabs)
            cutoff = jnp.concatenate([cutoffs_ref[own, :] for own in there], axis=0)
            change = (CODE_STEP * factor) * dot(atoms_at(ref, places, owned, reach), frames, ((1,), (0,)))
            first = (i * each + places[0]) * owned
            value = soft(values_ref[first : first + change.shape[0], :].astype(F32) + change, cutoff).astype(BF16)
            for b, own in enumerate(there):
                codes_out[own, :] = value[b * owned : (b + 1) * owned]
    gradient_ref[...] = jnp.zeros_like(gradient_ref)

    def body(n):
        gradient_ref[...] += dot(kept_ref[n + 1], windows_of(hankel_ref, n, width), ((1,), (0,)))

    repeat(slabs, body)
    atoms = kept_ref[slabs + 1].astype(F32) + kept_ref[slabs + 2].astype(F32)
    atoms_out[...] = normalised(atoms + factor * gradient_ref[...])
    rows_ref[: slabs * per, :] = residual
    residual_out[...] = rows_ref[pl.ds(me * per, per), :]


def call(kernel, outs, scratch, *args):
    vmem = pl.BlockSpec(memory_space=pltpu.VMEM)
    room = sum(math.prod(a.shape) * jnp.dtype(a.dtype).itemsize for a in [*args, *outs, *scratch])
    return pl.pallas_call(
        kernel,
        out_shape=tuple(outs),
        in_specs=[pl.BlockSpec(memory_space=pltpu.SMEM)] + [vmem] * (len(args) - 1),
        out_specs=(vmem,) * len(outs),
        scratch_shapes=scratch,
        compiler_params=pltpu.CompilerParams(vmem_limit_bytes=room + 6 * 1024 * 1024),
    )(*args)


def swapped(block, distance):
    count = lax.axis_size("tm")
    return lax.ppermute(block, "tm", [(i, i ^ distance) for i in range(count)])


def tied(value, *others):
    return lax.optimization_barrier((value, others))[0]


def exchanged(block, part, alone, late={}):
    distance = lax.axis_size("tm") // 2
    rows = part.shape[0]
    buffers = [block]
    while True:
        high = lax.reduce_precision(part, 8, 7)
        low = lax.reduce_precision(part - high, 8, 7)
        sent = [high.astype(BF16), low.astype(BF16)]
        if distance > alone:
            sent = buffers + sent
        sent = jnp.concatenate(sent)
        if distance in late:
            sent = tied(sent, late[distance])
        other = swapped(sent, distance)
        end = sent.shape[0] - 2 * rows
        if distance > alone:
            buffers = [sent[:end], other[:end]]
            whole = [sent, other]
        if distance == 1:
            return buffers, whole, (sent, other)
        part = (high + low) + (other[end : end + rows].astype(F32) + other[end + rows :].astype(F32))
        distance //= 2


def on_device(signal, codes, dictionary, thresholds):
    _, atom_count, width = codes.shape
    owned, lag_count = dictionary.shape
    slabs = lax.axis_size("tm")
    per = width // LANES
    blocks = slabs * per
    factor = (atom_count * lag_count) ** (-0.5)
    me = lax.axis_index("tm")
    at = me.astype(jnp.int32).reshape(1)
    signal_rows = signal.reshape(per, LANES)
    own_thresholds = lax.dynamic_slice(thresholds, (me * owned,), (owned,)).reshape(owned, 1)
    codes = codes[0]

    by_atom = lax.all_to_all(codes.reshape(slabs, owned, width), "tm", 0, 0, tiled=True)

    sums = [pltpu.VMEM((LANES, LANES), F32), pltpu.VMEM((blocks, 8, LANES), F32)]
    windows = [
        pltpu.VMEM((blocks + 8, LANES), F32),
        pltpu.VMEM((blocks + 8, 8, LANES), F32),
        pltpu.VMEM((blocks + per - 1, LANES, LANES), BF16),
        pltpu.VMEM((owned, lag_count), F32),
    ]
    atoms_shape = jax.ShapeDtypeStruct((owned, lag_count), F32)
    taps_shape = jax.ShapeDtypeStruct((owned * lag_count // LANES, LANES), BF16)
    part_shape = jax.ShapeDtypeStruct((blocks, LANES), F32)
    taps, part = call(
        functools.partial(first_kernel, factor), (taps_shape, part_shape), sums, at, dictionary, by_atom, signal_rows
    )
    before, _, first = exchanged(taps, part, 2)
    kept = slabs + 3 + pl.cdiv((2 * per - 1) * (LANES // owned), per)
    taps, kept, part = call(
        functools.partial(second_kernel, factor),
        [taps_shape, jax.ShapeDtypeStruct((kept, owned, width), BF16), part_shape],
        windows + sums,
        at, *first, dictionary, by_atom, own_thresholds, signal_rows,
    )
    all_thresholds = thresholds.reshape(-1, LANES)
    cutoffs = pltpu.VMEM((atom_count, 1), F32)
    mine = jnp.concatenate(before)
    other = swapped(tied(mine, part), 2)
    before = [mine, other, swapped(mine, 1), swapped(other, 1)]
    (values,) = call(
        functools.partial(shrink_kernel, factor, owned),
        [jax.ShapeDtypeStruct((atom_count, width), F32)],
        [cutoffs],
        at, kept, codes, all_thresholds, *before,
    )
    _, after, second = exchanged(taps, part, 1, {4: other, 1: values})
    after = after + [swapped(buffer, 1) for buffer in after]
    atoms, residual, codes = call(
        functools.partial(third_kernel, factor),
        [
            atoms_shape,
            jax.ShapeDtypeStruct((per, LANES), F32),
            jax.ShapeDtypeStruct((atom_count, width), BF16),
        ],
        [*windows, cutoffs],
        at, *second, kept, values, all_thresholds, *after,
    )
    return codes[None], atoms, residual.reshape(1, width)


def solution(mesh):
    return jax.shard_map(
        on_device,
        mesh=mesh,
        in_specs=(P("groups", "tm"), P("groups", None, "tm"), P("tm", None), P()),
        out_specs=(P("groups", None, "tm"), P(("groups", "tm"), None), P("groups", "tm")),
        check_vma=False,
    )
```

```python
import functools
import math

import jax
import jax.numpy as jnp
from jax import lax
from jax.experimental import pallas as pl
from jax.experimental.pallas import tpu as pltpu
from jax.sharding import PartitionSpec as P

CODE_STEP = 6.0
EPSILON = 1e-06
LANES = 128
F32, BF16 = jnp.float32, jnp.bfloat16


def dot(a, b, dims):
    return lax.dot_general(a, b, (dims, ((), ())), preferred_element_type=F32)


def repeat(count, body, carry=None):
    def step(i, carry):
        return body(i) if carry is None else body(i, carry)

    if count > 80:
        return lax.fori_loop(0, count, step, carry)
    for i in range(count):
        carry = step(i, carry)
    return carry


def row_lane():
    shape = (LANES, LANES)
    return lax.broadcasted_iota(jnp.int32, shape, 0), lax.broadcasted_iota(jnp.int32, shape, 1)


def turn_rows(rows_ref, turned_ref, count):
    q = lax.broadcasted_iota(jnp.int32, (8, LANES), 0)

    def turn(m):
        group = jnp.broadcast_to(rows_ref[pl.ds(m, 1), :], (8, LANES))
        for bit in (1, 2, 4):
            group = jnp.where((q & bit) != 0, pltpu.roll(group, LANES - bit, 1), group)
        turned_ref[m] = group

    repeat(count, turn)


def fill_hankel(turned_ref, hankel_ref, first, count):
    q = lax.broadcasted_iota(jnp.int32, (8, LANES), 0)
    v = lax.broadcasted_iota(jnp.int32, (8, LANES), 1)
    for a in range(0, LANES, 16):
        keeps = [q + v + (a + b) < LANES for b in (0, 8)]

        def groups(m):
            group = turned_ref[m]
            return [pltpu.roll(group, LANES - a - b, 1) if a + b else group for b in (0, 8)]

        here = groups(first)
        for m in range(first, first + count):
            after = groups(m + 1)
            pair = [jnp.where(keep, old, new) for keep, old, new in zip(keeps, here, after)]
            hankel_ref[m, a : a + 16, :] = jnp.concatenate(pair, axis=0).astype(BF16)
            here = after


def over_slabs(turned_ref, hankel_ref, slabs, per, body):
    fill_hankel(turned_ref, hankel_ref, 0, 2 * per - 1)
    for n in range(slabs):
        if n + 1 < slabs:
            fill_hankel(turned_ref, hankel_ref, (n + 2) * per - 1, per)
        body(n)


def windows_of(hankel_ref, slab, width):
    per = width // LANES
    rows = [
        jnp.concatenate([hankel_ref[slab * per + p + i] for i in range(per)], axis=1)
        for p in range(per)
    ]
    return jnp.concatenate(rows, axis=0)


def soft(value, cutoff):
    return value - jnp.minimum(jnp.maximum(value, -cutoff), cutoff)


def normalised(updated):
    return updated / jnp.sqrt(jnp.mean(updated * updated, axis=1, keepdims=True) + EPSILON)


def stacked_taps(atoms):
    return jnp.concatenate([atoms[:, i : i + LANES] for i in range(0, atoms.shape[1], LANES)], axis=0)


def rebuild(taps, slab_of, slabs, width, turned_ref, sums_ref):
    per = width // LANES
    q, v = row_lane()
    keep = v >= q
    turned_ref[...] = jnp.zeros_like(turned_ref)

    def body(n):
        now, before = slab_of(n), slab_of(n - 1)
        shifted = [now] + [
            jnp.concatenate([before[:, width - LANES * p :], now[:, : width - LANES * p]], axis=1) for p in range(1, per)
        ]
        products = dot(taps, jnp.concatenate(shifted, axis=0), ((0,), (0,)))
        last = turned_ref[...]
        for i in range(per):
            turned = pltpu.roll(products[:, LANES * i : LANES * (i + 1)], 0, 1, stride=1, stride_axis=0)
            placed = jnp.where(keep, turned, last)
            sums_ref[n * per + i] = placed.reshape(LANES // 8, 8, LANES).sum(axis=0)
            last = turned
        turned_ref[...] = last

    repeat(slabs, body)


def partial_residual(me, factor, signal_ref, sums_ref, out_ref):
    rows = signal_ref.shape[0]
    out_ref[...] = -factor * jnp.sum(sums_ref[...], axis=1)
    own = pl.ds(me * rows, rows)
    out_ref[own, :] = out_ref[own, :] + signal_ref[...]


def owner_of(me, place, count):
    distance, bit = count // 2, 0
    while distance:
        if place >> bit & 1:
            me = me ^ distance
        distance, bit = distance // 2, bit + 1
    return me


def first_kernel(factor, me_ref, atoms_ref, codes_ref, signal_ref, taps_out, part_out, turned_ref, sums_ref):
    slabs, owned, width = codes_ref.shape
    taps = stacked_taps(atoms_ref[...].astype(BF16))
    taps_out[...] = taps
    zero = jnp.zeros((owned, width), BF16)

    def slab_of(n):
        if isinstance(n, int):
            return codes_ref[n] if n >= 0 else zero
        return jnp.where(n >= 0, codes_ref[jnp.maximum(n, 0)], zero)

    rebuild(taps, slab_of, slabs, width, turned_ref, sums_ref)
    partial_residual(me_ref[0], factor, signal_ref, sums_ref, part_out)


def whole_residual(terms):
    rows = terms[0].shape[0] // 2
    mine, other = (ref[:rows, :].astype(F32) + ref[rows:, :].astype(F32) for ref in terms)
    return mine + other


def round_rows(residual, rows_ref):
    count = residual.shape[0]
    rows_ref[:count, :] = residual.astype(BF16).astype(F32)
    rows_ref[count:, :] = jnp.zeros((rows_ref.shape[0] - count, LANES), F32)


def kept_at(piece, slabs, per):
    lane = piece % per * LANES
    return slabs + 3 + piece // per, slice(lane, lane + LANES)


def second_kernel(
    factor, me_ref, sent_ref, other_ref, atoms_ref, codes_ref, thresholds_ref, signal_ref,
    taps_out, codes_out, part_out,
    rows_ref, turned_rows_ref, hankel_ref, gradient_ref, turned_ref, sums_ref,
):
    slabs, owned, width = codes_ref.shape
    per = width // LANES
    round_rows(whole_residual((sent_ref, other_ref)), rows_ref)
    turn_rows(rows_ref, turned_rows_ref, hankel_ref.shape[0] + 1)
    atoms = atoms_ref[...]
    atoms_b = atoms.astype(BF16)
    cutoff = CODE_STEP * thresholds_ref[...]
    gradient_ref[...] = jnp.zeros_like(gradient_ref)
    codes_out[0] = jnp.zeros((owned, width), BF16)

    def body(n):
        frames = windows_of(hankel_ref, n, width)
        code = codes_ref[n]
        both = dot(jnp.concatenate([atoms_b, code], axis=0), frames, ((1,), (0,)))
        gradient_ref[...] += both[owned:]
        value = code.astype(F32) + (CODE_STEP * factor) * both[:owned]
        codes_out[n + 1] = soft(value, cutoff).astype(BF16)

    over_slabs(turned_rows_ref, hankel_ref, slabs, per, body)
    for m in range(2 * per - 1):
        block = hankel_ref[me_ref[0] * per + m]
        for h in range(LANES // owned):
            slab, lane = kept_at(m * (LANES // owned) + h, slabs, per)
            codes_out[slab, :, lane] = block[h * owned : (h + 1) * owned, :]
    after = normalised(atoms + factor * gradient_ref[...])
    after_b = after.astype(BF16)
    codes_out[slabs + 1] = after_b
    codes_out[slabs + 2] = (after - after_b.astype(F32)).astype(BF16)
    taps = stacked_taps(after_b)
    taps_out[...] = taps
    rebuild(taps, lambda n: codes_out[n + 1], slabs, width, turned_ref, sums_ref)
    partial_residual(me_ref[0], factor, signal_ref, sums_ref, part_out)


def atoms_at(ref, places, owned, reach):
    taps = [[ref[(b * reach + p) * owned : (b * reach + p + 1) * owned, :] for p in range(reach)] for b in places]
    return jnp.concatenate([jnp.concatenate(row, axis=1) for row in taps], axis=0)


def rows_at(me, first, places, owned, count):
    return [pl.ds(pl.multiple_of(owner_of(me, first + b, count) * owned, owned), owned) for b in places]


def batches(each, owned):
    together = max(1, min(each, 256 // owned))
    return [range(start, start + together) for start in range(0, each, together)]


def spread(thresholds_ref, cutoffs_ref):
    count = thresholds_ref.shape[0]
    filled = jnp.concatenate([thresholds_ref[...], jnp.zeros((LANES - count, LANES), F32)], axis=0)
    columns = CODE_STEP * filled.T
    for m in range(count):
        cutoffs_ref[m * LANES : (m + 1) * LANES, :] = columns[:, m : m + 1]


def shrink_kernel(factor, owned, me_ref, kept_ref, codes_ref, thresholds_ref, *refs):
    buffers, values_out, cutoffs_ref = refs[:-2], refs[-2], refs[-1]
    atom_count, width = codes_ref.shape
    slabs, per, reach = atom_count // owned, width // LANES, width // LANES
    spread(thresholds_ref, cutoffs_ref)
    each = LANES // owned
    pieces = [kept_at(piece, slabs, per) for piece in range((2 * per - 1) * each)]
    pieces = [kept_ref[slab, :, lane] for slab, lane in pieces]
    frames = windows_of([jnp.concatenate(pieces[i : i + each], axis=0) for i in range(0, len(pieces), each)], 0, width)
    each = slabs // len(buffers)
    for i, ref in enumerate(buffers):
        for places in batches(each, owned):
            there = rows_at(me_ref[0], i * each, places, owned, slabs)
            value = jnp.concatenate([codes_ref[own, :] for own in there], axis=0).astype(F32)
            cutoff = jnp.concatenate([cutoffs_ref[own, :] for own in there], axis=0)
            value += (CODE_STEP * factor) * dot(atoms_at(ref, places, owned, reach), frames, ((1,), (0,)))
            first = (i * each + places[0]) * owned
            values_out[first : first + value.shape[0], :] = soft(value, cutoff).astype(values_out.dtype)


def third_kernel(factor, me_ref, sent_ref, other_ref, kept_ref, values_ref, thresholds_ref, *refs):
    buffers = refs[:-8]
    atoms_out, residual_out, codes_out, rows_ref, turned_rows_ref, hankel_ref, gradient_ref, cutoffs_ref = refs[-8:]
    owned, lag_count = atoms_out.shape
    atom_count, width = values_ref.shape
    slabs, per, reach = atom_count // owned, width // LANES, lag_count // LANES
    me = me_ref[0]
    residual = whole_residual((sent_ref, other_ref))
    round_rows(residual, rows_ref)
    turn_rows(rows_ref, turned_rows_ref, hankel_ref.shape[0] + 1)
    spread(thresholds_ref, cutoffs_ref)
    gradient_ref[...] = jnp.zeros_like(gradient_ref)

    def body(n):
        gradient_ref[...] += dot(kept_ref[n + 1], windows_of(hankel_ref, n, width), ((1,), (0,)))

    over_slabs(turned_rows_ref, hankel_ref, slabs, per, body)
    atoms = kept_ref[slabs + 1].astype(F32) + kept_ref[slabs + 2].astype(F32)
    atoms_out[...] = normalised(atoms + factor * gradient_ref[...])
    rows_ref[: slabs * per, :] = residual
    residual_out[...] = rows_ref[pl.ds(me * per, per), :]
    frames = windows_of(hankel_ref, me, width)
    each = slabs // len(buffers)
    for i, ref in enumerate(buffers):
        for places in batches(each, owned):
            there = rows_at(me, i * each, places, owned, slabs)
            cutoff = jnp.concatenate([cutoffs_ref[own, :] for own in there], axis=0)
            change = (CODE_STEP * factor) * dot(atoms_at(ref, places, owned, reach), frames, ((1,), (0,)))
            first = (i * each + places[0]) * owned
            value = soft(values_ref[first : first + change.shape[0], :].astype(F32) + change, cutoff).astype(BF16)
            for b, own in enumerate(there):
                codes_out[own, :] = value[b * owned : (b + 1) * owned]


def call(kernel, outs, scratch, *args):
    vmem = pl.BlockSpec(memory_space=pltpu.VMEM)
    room = sum(math.prod(a.shape) * jnp.dtype(a.dtype).itemsize for a in [*args, *outs, *scratch])
    return pl.pallas_call(
        kernel,
        out_shape=tuple(outs),
        in_specs=[pl.BlockSpec(memory_space=pltpu.SMEM)] + [vmem] * (len(args) - 1),
        out_specs=(vmem,) * len(outs),
        scratch_shapes=scratch,
        compiler_params=pltpu.CompilerParams(vmem_limit_bytes=room + 6 * 1024 * 1024),
    )(*args)


def swapped(block, distance):
    count = lax.axis_size("tm")
    return lax.ppermute(block, "tm", [(i, i ^ distance) for i in range(count)])


def tied(value, *others):
    return lax.optimization_barrier((value, others))[0]


def exchanged(block, part, alone, late={}):
    distance = lax.axis_size("tm") // 2
    rows = part.shape[0]
    buffers = [block]
    while True:
        high = lax.reduce_precision(part, 8, 7)
        low = lax.reduce_precision(part - high, 8, 7)
        sent = [high.astype(BF16), low.astype(BF16)]
        if distance > alone:
            sent = buffers + sent
        sent = jnp.concatenate(sent)
        if distance in late:
            sent = tied(sent, late[distance])
        other = swapped(sent, distance)
        end = sent.shape[0] - 2 * rows
        if distance > alone:
            buffers = [sent[:end], other[:end]]
            whole = [sent, other]
        if distance == 1:
            return buffers, whole, (sent, other)
        part = (high + low) + (other[end : end + rows].astype(F32) + other[end + rows :].astype(F32))
        distance //= 2


def on_device(signal, codes, dictionary, thresholds):
    _, atom_count, width = codes.shape
    owned, lag_count = dictionary.shape
    slabs = lax.axis_size("tm")
    per = width // LANES
    blocks = slabs * per
    factor = (atom_count * lag_count) ** (-0.5)
    me = lax.axis_index("tm")
    at = me.astype(jnp.int32).reshape(1)
    signal_rows = signal.reshape(per, LANES)
    own_thresholds = lax.dynamic_slice(thresholds, (me * owned,), (owned,)).reshape(owned, 1)
    codes = codes[0]

    by_atom = lax.all_to_all(codes.reshape(slabs, owned, width), "tm", 0, 0, tiled=True)

    sums = [pltpu.VMEM((LANES, LANES), F32), pltpu.VMEM((blocks, 8, LANES), F32)]
    windows = [
        pltpu.VMEM((blocks + 8, LANES), F32),
        pltpu.VMEM((blocks + 8, 8, LANES), F32),
        pltpu.VMEM((blocks + per - 1, LANES, LANES), BF16),
        pltpu.VMEM((owned, lag_count), F32),
    ]
    atoms_shape = jax.ShapeDtypeStruct((owned, lag_count), F32)
    taps_shape = jax.ShapeDtypeStruct((owned * lag_count // LANES, LANES), BF16)
    part_shape = jax.ShapeDtypeStruct((blocks, LANES), F32)
    taps, part = call(
        functools.partial(first_kernel, factor), (taps_shape, part_shape), sums, at, dictionary, by_atom, signal_rows
    )
    before, _, first = exchanged(taps, part, 2)
    kept = slabs + 3 + pl.cdiv((2 * per - 1) * (LANES // owned), per)
    taps, kept, part = call(
        functools.partial(second_kernel, factor),
        [taps_shape, jax.ShapeDtypeStruct((kept, owned, width), BF16), part_shape],
        windows + sums,
        at, *first, dictionary, by_atom, own_thresholds, signal_rows,
    )
    all_thresholds = thresholds.reshape(-1, LANES)
    cutoffs = pltpu.VMEM((atom_count, 1), F32)
    mine = jnp.concatenate(before)
    other = swapped(tied(mine, part), 2)
    before = [mine, other, swapped(mine, 1), swapped(other, 1)]
    (values,) = call(
        functools.partial(shrink_kernel, factor, owned),
        [jax.ShapeDtypeStruct((atom_count, width), F32)],
        [cutoffs],
        at, kept, codes, all_thresholds, *before,
    )
    _, after, second = exchanged(taps, part, 1, {4: other, 1: values})
    after = after + [swapped(buffer, 1) for buffer in after]
    atoms, residual, codes = call(
        functools.partial(third_kernel, factor),
        [
            atoms_shape,
            jax.ShapeDtypeStruct((per, LANES), F32),
            jax.ShapeDtypeStruct((atom_count, width), BF16),
        ],
        [*windows, cutoffs],
        at, *second, kept, values, all_thresholds, *after,
    )
    return codes[None], atoms, residual.reshape(1, width)


def solution(mesh):
    return jax.shard_map(
        on_device,
        mesh=mesh,
        in_specs=(P("groups", "tm"), P("groups", None, "tm"), P("tm", None), P()),
        out_specs=(P("groups", None, "tm"), P(("groups", "tm"), None), P("groups", "tm")),
        check_vma=False,
    )
```

```python
import functools
import math

import jax
import jax.numpy as jnp
from jax import lax
from jax.experimental import pallas as pl
from jax.experimental.pallas import tpu as pltpu
from jax.sharding import PartitionSpec as P

CODE_STEP = 6.0
EPSILON = 1e-06
LANES = 128
F32, BF16 = jnp.float32, jnp.bfloat16


def dot(a, b, dims):
    return lax.dot_general(a, b, (dims, ((), ())), preferred_element_type=F32)


def repeat(count, body, carry=None):
    def step(i, carry):
        return body(i) if carry is None else body(i, carry)

    if count > 80:
        return lax.fori_loop(0, count, step, carry)
    for i in range(count):
        carry = step(i, carry)
    return carry


def row_lane():
    shape = (LANES, LANES)
    return lax.broadcasted_iota(jnp.int32, shape, 0), lax.broadcasted_iota(jnp.int32, shape, 1)


def turn_rows(rows_ref, turned_ref, count):
    q = lax.broadcasted_iota(jnp.int32, (8, LANES), 0)

    def turn(m):
        group = jnp.broadcast_to(rows_ref[pl.ds(m, 1), :], (8, LANES))
        for bit in (1, 2, 4):
            group = jnp.where((q & bit) != 0, pltpu.roll(group, LANES - bit, 1), group)
        turned_ref[m] = group

    repeat(count, turn)


def fill_hankel(turned_ref, hankel_ref, first, count):
    q = lax.broadcasted_iota(jnp.int32, (8, LANES), 0)
    v = lax.broadcasted_iota(jnp.int32, (8, LANES), 1)
    for a in range(0, LANES, 16):
        keeps = [q + v + (a + b) < LANES for b in (0, 8)]

        def groups(m):
            group = turned_ref[m]
            return [pltpu.roll(group, LANES - a - b, 1) if a + b else group for b in (0, 8)]

        here = groups(first)
        for m in range(first, first + count):
            after = groups(m + 1)
            pair = [jnp.where(keep, old, new) for keep, old, new in zip(keeps, here, after)]
            hankel_ref[m, a : a + 16, :] = jnp.concatenate(pair, axis=0).astype(BF16)
            here = after


def over_slabs(turned_ref, hankel_ref, slabs, per, body):
    fill_hankel(turned_ref, hankel_ref, 0, 2 * per - 1)
    for n in range(slabs):
        if n + 1 < slabs:
            fill_hankel(turned_ref, hankel_ref, (n + 2) * per - 1, per)
        body(n)


def windows_of(hankel_ref, slab, width):
    per = width // LANES
    rows = [
        jnp.concatenate([hankel_ref[slab * per + p + i] for i in range(per)], axis=1)
        for p in range(per)
    ]
    return jnp.concatenate(rows, axis=0)


def soft(value, cutoff):
    return value - jnp.minimum(jnp.maximum(value, -cutoff), cutoff)


def normalised(updated):
    return updated / jnp.sqrt(jnp.mean(updated * updated, axis=1, keepdims=True) + EPSILON)


def stacked_taps(atoms):
    return jnp.concatenate([atoms[:, i : i + LANES] for i in range(0, atoms.shape[1], LANES)], axis=0)


def delayed(now, before):
    width = now.shape[1]
    rows = [now]
    for late in range(LANES, width, LANES):
        rows.append(jnp.concatenate([before[:, width - late :], now[:, : width - late]], axis=1))
    return jnp.concatenate(rows, axis=0)


def rebuild(taps, slab_of, slabs, width, turned_ref, sums_ref):
    per = width // LANES
    q, v = row_lane()
    keep = v >= q
    turned_ref[...] = jnp.zeros_like(turned_ref)

    def body(n):
        now, before = slab_of(n), slab_of(n - 1)
        products = dot(taps, delayed(now, before), ((0,), (0,)))
        last = turned_ref[...]
        for i in range(per):
            turned = pltpu.roll(products[:, LANES * i : LANES * (i + 1)], 0, 1, stride=1, stride_axis=0)
            placed = jnp.where(keep, turned, last)
            sums_ref[n * per + i] = placed.reshape(LANES // 8, 8, LANES).sum(axis=0)
            last = turned
        turned_ref[...] = last

    repeat(slabs, body)


def partial_residual(me, factor, signal_ref, sums_ref, out_ref):
    rows = signal_ref.shape[0]
    out_ref[...] = -factor * jnp.sum(sums_ref[...], axis=1)
    own = pl.ds(me * rows, rows)
    out_ref[own, :] = out_ref[own, :] + signal_ref[...]


def owner_of(me, place, count):
    distance, bit = count // 2, 0
    while distance:
        if place >> bit & 1:
            me = me ^ distance
        distance, bit = distance // 2, bit + 1
    return me


def first_kernel(factor, me_ref, atoms_ref, codes_ref, signal_ref, taps_out, part_out, turned_ref, sums_ref):
    slabs, owned, width = codes_ref.shape
    taps = stacked_taps(atoms_ref[...].astype(BF16))
    taps_out[...] = taps
    zero = jnp.zeros((owned, width), BF16)

    def slab_of(n):
        if isinstance(n, int):
            return codes_ref[n] if n >= 0 else zero
        return jnp.where(n >= 0, codes_ref[jnp.maximum(n, 0)], zero)

    rebuild(taps, slab_of, slabs, width, turned_ref, sums_ref)
    partial_residual(me_ref[0], factor, signal_ref, sums_ref, part_out)


def whole_residual(terms):
    rows = terms[0].shape[0] // 2
    mine, other = (ref[:rows, :].astype(F32) + ref[rows:, :].astype(F32) for ref in terms)
    return mine + other


def round_rows(residual, rows_ref):
    count = residual.shape[0]
    rows_ref[:count, :] = residual.astype(BF16).astype(F32)
    rows_ref[count:, :] = jnp.zeros((rows_ref.shape[0] - count, LANES), F32)


def kept_at(piece, slabs, per):
    lane = piece % per * LANES
    return slabs + 3 + piece // per, slice(lane, lane + LANES)


def second_kernel(
    factor, me_ref, sent_ref, other_ref, atoms_ref, codes_ref, thresholds_ref, signal_ref,
    taps_out, codes_out, part_out,
    rows_ref, turned_rows_ref, hankel_ref, gradient_ref, turned_ref, sums_ref,
):
    slabs, owned, width = codes_ref.shape
    per = width // LANES
    round_rows(whole_residual((sent_ref, other_ref)), rows_ref)
    turn_rows(rows_ref, turned_rows_ref, hankel_ref.shape[0] + 1)
    atoms = atoms_ref[...]
    atoms_b = atoms.astype(BF16)
    cutoff = CODE_STEP * thresholds_ref[...]
    gradient_ref[...] = jnp.zeros_like(gradient_ref)
    codes_out[0] = jnp.zeros((owned, width), BF16)

    def body(n):
        frames = windows_of(hankel_ref, n, width)
        code = codes_ref[n]
        both = dot(jnp.concatenate([atoms_b, code], axis=0), frames, ((1,), (0,)))
        gradient_ref[...] += both[owned:]
        value = code.astype(F32) + (CODE_STEP * factor) * both[:owned]
        codes_out[n + 1] = soft(value, cutoff).astype(BF16)

    over_slabs(turned_rows_ref, hankel_ref, slabs, per, body)
    for m in range(2 * per - 1):
        block = hankel_ref[me_ref[0] * per + m]
        for h in range(LANES // owned):
            slab, lane = kept_at(m * (LANES // owned) + h, slabs, per)
            codes_out[slab, :, lane] = block[h * owned : (h + 1) * owned, :]
    after = normalised(atoms + factor * gradient_ref[...])
    after_b = after.astype(BF16)
    codes_out[slabs + 1] = after_b
    codes_out[slabs + 2] = (after - after_b.astype(F32)).astype(BF16)
    taps = stacked_taps(after_b)
    taps_out[...] = taps
    rebuild(taps, lambda n: codes_out[n + 1], slabs, width, turned_ref, sums_ref)
    partial_residual(me_ref[0], factor, signal_ref, sums_ref, part_out)


def atoms_at(ref, places, owned, reach):
    taps = [[ref[(b * reach + p) * owned : (b * reach + p + 1) * owned, :] for p in range(reach)] for b in places]
    return jnp.concatenate([jnp.concatenate(row, axis=1) for row in taps], axis=0)


def rows_at(me, first, places, owned, count):
    return [pl.ds(pl.multiple_of(owner_of(me, first + b, count) * owned, owned), owned) for b in places]


def batches(each, owned):
    together = max(1, min(each, 256 // owned))
    return [range(start, start + together) for start in range(0, each, together)]


def spread(thresholds_ref, cutoffs_ref):
    count = thresholds_ref.shape[0]
    filled = jnp.concatenate([thresholds_ref[...], jnp.zeros((LANES - count, LANES), F32)], axis=0)
    columns = CODE_STEP * filled.T
    for m in range(count):
        cutoffs_ref[m * LANES : (m + 1) * LANES, :] = columns[:, m : m + 1]


def shrink_kernel(factor, owned, me_ref, kept_ref, codes_ref, thresholds_ref, *refs):
    buffers, values_out, cutoffs_ref = refs[:-2], refs[-2], refs[-1]
    atom_count, width = codes_ref.shape
    slabs, per, reach = atom_count // owned, width // LANES, width // LANES
    spread(thresholds_ref, cutoffs_ref)
    each = LANES // owned
    pieces = [kept_at(piece, slabs, per) for piece in range((2 * per - 1) * each)]
    pieces = [kept_ref[slab, :, lane] for slab, lane in pieces]
    frames = windows_of([jnp.concatenate(pieces[i : i + each], axis=0) for i in range(0, len(pieces), each)], 0, width)
    each = slabs // len(buffers)
    for i, ref in enumerate(buffers):
        for places in batches(each, owned):
            there = rows_at(me_ref[0], i * each, places, owned, slabs)
            value = jnp.concatenate([codes_ref[own, :] for own in there], axis=0).astype(F32)
            cutoff = jnp.concatenate([cutoffs_ref[own, :] for own in there], axis=0)
            value += (CODE_STEP * factor) * dot(atoms_at(ref, places, owned, reach), frames, ((1,), (0,)))
            first = (i * each + places[0]) * owned
            values_out[first : first + value.shape[0], :] = soft(value, cutoff).astype(values_out.dtype)


def third_kernel(factor, me_ref, sent_ref, other_ref, kept_ref, values_ref, thresholds_ref, *refs):
    buffers = refs[:-8]
    atoms_out, residual_out, codes_out, rows_ref, turned_rows_ref, hankel_ref, gradient_ref, cutoffs_ref = refs[-8:]
    owned, lag_count = atoms_out.shape
    atom_count, width = values_ref.shape
    slabs, per, reach = atom_count // owned, width // LANES, lag_count // LANES
    me = me_ref[0]
    residual = whole_residual((sent_ref, other_ref))
    round_rows(residual, rows_ref)
    turn_rows(rows_ref, turned_rows_ref, hankel_ref.shape[0] + 1)
    spread(thresholds_ref, cutoffs_ref)
    gradient_ref[...] = jnp.zeros_like(gradient_ref)

    def body(n):
        blocks = [hankel_ref[n * per + i] for i in range(per)]
        gradient_ref[...] += dot(delayed(kept_ref[n + 1], kept_ref[n]), jnp.concatenate(blocks, axis=0), ((1,), (0,)))

    over_slabs(turned_rows_ref, hankel_ref, slabs, per, body)
    gradient = jnp.concatenate([gradient_ref[p * owned : (p + 1) * owned, :] for p in range(reach)], axis=1)
    atoms = kept_ref[slabs + 1].astype(F32) + kept_ref[slabs + 2].astype(F32)
    atoms_out[...] = normalised(atoms + factor * gradient)
    rows_ref[: slabs * per, :] = residual
    residual_out[...] = rows_ref[pl.ds(me * per, per), :]
    frames = windows_of(hankel_ref, me, width)
    each = slabs // len(buffers)
    for i, ref in enumerate(buffers):
        for places in batches(each, owned):
            there = rows_at(me, i * each, places, owned, slabs)
            cutoff = jnp.concatenate([cutoffs_ref[own, :] for own in there], axis=0)
            change = (CODE_STEP * factor) * dot(atoms_at(ref, places, owned, reach), frames, ((1,), (0,)))
            first = (i * each + places[0]) * owned
            value = soft(values_ref[first : first + change.shape[0], :].astype(F32) + change, cutoff).astype(BF16)
            for b, own in enumerate(there):
                codes_out[own, :] = value[b * owned : (b + 1) * owned]


def call(kernel, outs, scratch, *args):
    vmem = pl.BlockSpec(memory_space=pltpu.VMEM)
    room = sum(math.prod(a.shape) * jnp.dtype(a.dtype).itemsize for a in [*args, *outs, *scratch])
    return pl.pallas_call(
        kernel,
        out_shape=tuple(outs),
        in_specs=[pl.BlockSpec(memory_space=pltpu.SMEM)] + [vmem] * (len(args) - 1),
        out_specs=(vmem,) * len(outs),
        scratch_shapes=scratch,
        compiler_params=pltpu.CompilerParams(vmem_limit_bytes=room + 6 * 1024 * 1024),
    )(*args)


def swapped(block, distance):
    count = lax.axis_size("tm")
    return lax.ppermute(block, "tm", [(i, i ^ distance) for i in range(count)])


def tied(value, *others):
    return lax.optimization_barrier((value, others))[0]


def exchanged(block, part, alone, late={}):
    distance = lax.axis_size("tm") // 2
    rows = part.shape[0]
    buffers = [block]
    while True:
        high = lax.reduce_precision(part, 8, 7)
        low = lax.reduce_precision(part - high, 8, 7)
        sent = [high.astype(BF16), low.astype(BF16)]
        if distance > alone:
            sent = buffers + sent
        sent = jnp.concatenate(sent)
        if distance in late:
            sent = tied(sent, late[distance])
        other = swapped(sent, distance)
        end = sent.shape[0] - 2 * rows
        if distance > alone:
            buffers = [sent[:end], other[:end]]
            whole = [sent, other]
        if distance == 1:
            return buffers, whole, (sent, other)
        part = (high + low) + (other[end : end + rows].astype(F32) + other[end + rows :].astype(F32))
        distance //= 2


def on_device(signal, codes, dictionary, thresholds):
    _, atom_count, width = codes.shape
    owned, lag_count = dictionary.shape
    slabs = lax.axis_size("tm")
    per = width // LANES
    blocks = slabs * per
    factor = (atom_count * lag_count) ** (-0.5)
    me = lax.axis_index("tm")
    at = me.astype(jnp.int32).reshape(1)
    signal_rows = signal.reshape(per, LANES)
    own_thresholds = lax.dynamic_slice(thresholds, (me * owned,), (owned,)).reshape(owned, 1)
    codes = codes[0]

    by_atom = lax.all_to_all(codes.reshape(slabs, owned, width), "tm", 0, 0, tiled=True)

    sums = [pltpu.VMEM((LANES, LANES), F32), pltpu.VMEM((blocks, 8, LANES), F32)]
    windows = [
        pltpu.VMEM((blocks + 8, LANES), F32),
        pltpu.VMEM((blocks + 8, 8, LANES), F32),
        pltpu.VMEM((blocks + per - 1, LANES, LANES), BF16),
        pltpu.VMEM((owned, lag_count), F32),
    ]
    atoms_shape = jax.ShapeDtypeStruct((owned, lag_count), F32)
    taps_shape = jax.ShapeDtypeStruct((owned * lag_count // LANES, LANES), BF16)
    part_shape = jax.ShapeDtypeStruct((blocks, LANES), F32)
    taps, part = call(
        functools.partial(first_kernel, factor), (taps_shape, part_shape), sums, at, dictionary, by_atom, signal_rows
    )
    before, _, first = exchanged(taps, part, 2)
    kept = slabs + 3 + pl.cdiv((2 * per - 1) * (LANES // owned), per)
    taps, kept, part = call(
        functools.partial(second_kernel, factor),
        [taps_shape, jax.ShapeDtypeStruct((kept, owned, width), BF16), part_shape],
        windows + sums,
        at, *first, dictionary, by_atom, own_thresholds, signal_rows,
    )
    all_thresholds = thresholds.reshape(-1, LANES)
    cutoffs = pltpu.VMEM((atom_count, 1), F32)
    mine = jnp.concatenate(before)
    other = swapped(tied(mine, part), 2)
    before = [mine, other, swapped(mine, 1), swapped(other, 1)]
    (values,) = call(
        functools.partial(shrink_kernel, factor, owned),
        [jax.ShapeDtypeStruct((atom_count, width), F32)],
        [cutoffs],
        at, kept, codes, all_thresholds, *before,
    )
    _, after, second = exchanged(taps, part, 1, {4: other, 1: values})
    after = after + [swapped(buffer, 1) for buffer in after]
    atoms, residual, codes = call(
        functools.partial(third_kernel, factor),
        [
            atoms_shape,
            jax.ShapeDtypeStruct((per, LANES), F32),
            jax.ShapeDtypeStruct((atom_count, width), BF16),
        ],
        [*windows[:-1], pltpu.VMEM(taps_shape.shape, F32), cutoffs],
        at, *second, kept, values, all_thresholds, *after,
    )
    return codes[None], atoms, residual.reshape(1, width)


def solution(mesh):
    return jax.shard_map(
        on_device,
        mesh=mesh,
        in_specs=(P("groups", "tm"), P("groups", None, "tm"), P("tm", None), P()),
        out_specs=(P("groups", None, "tm"), P(("groups", "tm"), None), P("groups", "tm")),
        check_vma=False,
    )
```

```python
import functools
import math

import jax
import jax.numpy as jnp
from jax import lax
from jax.experimental import pallas as pl
from jax.experimental.pallas import tpu as pltpu
from jax.sharding import PartitionSpec as P

CODE_STEP = 6.0
EPSILON = 1e-06
LANES = 128
F32, BF16 = jnp.float32, jnp.bfloat16


def dot(a, b, dims):
    return lax.dot_general(a, b, (dims, ((), ())), preferred_element_type=F32)


def repeat(count, body, carry=None):
    def step(i, carry):
        return body(i) if carry is None else body(i, carry)

    if count > 80:
        return lax.fori_loop(0, count, step, carry)
    for i in range(count):
        carry = step(i, carry)
    return carry


def row_lane():
    shape = (LANES, LANES)
    return lax.broadcasted_iota(jnp.int32, shape, 0), lax.broadcasted_iota(jnp.int32, shape, 1)


def turn_rows(rows_ref, turned_ref, count):
    q = lax.broadcasted_iota(jnp.int32, (8, LANES), 0)

    def turn(m):
        group = jnp.broadcast_to(rows_ref[pl.ds(m, 1), :], (8, LANES))
        for bit in (1, 2, 4):
            group = jnp.where((q & bit) != 0, pltpu.roll(group, LANES - bit, 1), group)
        turned_ref[m] = group

    repeat(count, turn)


def fill_hankel(turned_ref, hankel_ref, first, count):
    q = lax.broadcasted_iota(jnp.int32, (8, LANES), 0)
    v = lax.broadcasted_iota(jnp.int32, (8, LANES), 1)
    for a in range(0, LANES, 16):
        keeps = [q + v + (a + b) < LANES for b in (0, 8)]

        def groups(m):
            group = turned_ref[m]
            return [pltpu.roll(group, LANES - a - b, 1) if a + b else group for b in (0, 8)]

        here = groups(first)
        for m in range(first, first + count):
            after = groups(m + 1)
            pair = [jnp.where(keep, old, new) for keep, old, new in zip(keeps, here, after)]
            hankel_ref[m, a : a + 16, :] = jnp.concatenate(pair, axis=0).astype(BF16)
            here = after


def over_slabs(turned_ref, hankel_ref, slabs, per, body):
    fill_hankel(turned_ref, hankel_ref, 0, 2 * per - 1)
    for n in range(slabs):
        if n + 1 < slabs:
            fill_hankel(turned_ref, hankel_ref, (n + 2) * per - 1, per)
        body(n)


def windows_of(hankel_ref, slab, width):
    per = width // LANES
    rows = [
        jnp.concatenate([hankel_ref[slab * per + p + i] for i in range(per)], axis=1)
        for p in range(per)
    ]
    return jnp.concatenate(rows, axis=0)


def soft(value, cutoff):
    return value - jnp.minimum(jnp.maximum(value, -cutoff), cutoff)


def normalised(updated):
    return updated / jnp.sqrt(jnp.mean(updated * updated, axis=1, keepdims=True) + EPSILON)


def stacked_taps(atoms):
    return jnp.concatenate([atoms[:, i : i + LANES] for i in range(0, atoms.shape[1], LANES)], axis=0)


def delayed(now, before):
    width = now.shape[1]
    rows = [now]
    for late in range(LANES, width, LANES):
        rows.append(jnp.concatenate([before[:, width - late :], now[:, : width - late]], axis=1))
    return jnp.concatenate(rows, axis=0)


def rebuild(taps, slab_of, slabs, width, sums_ref):
    per = width // LANES
    q, v = row_lane()
    keep = v >= q

    def body(n, last):
        now, before = slab_of(n), slab_of(n - 1)
        products = dot(taps, delayed(now, before), ((0,), (0,)))
        for i in range(per):
            turned = pltpu.roll(products[:, LANES * i : LANES * (i + 1)], 0, 1, stride=1, stride_axis=0)
            placed = jnp.where(keep, turned, last)
            sums_ref[n * per + i] = placed.reshape(LANES // 8, 8, LANES).sum(axis=0)
            last = turned
        return last

    repeat(slabs, body, jnp.zeros((LANES, LANES), F32))


def partial_residual(me, factor, signal_ref, sums_ref, out_ref):
    rows = signal_ref.shape[0]
    out_ref[...] = -factor * jnp.sum(sums_ref[...], axis=1)
    own = pl.ds(me * rows, rows)
    out_ref[own, :] = out_ref[own, :] + signal_ref[...]


def owner_of(me, place, count):
    distance, bit = count // 2, 0
    while distance:
        if place >> bit & 1:
            me = me ^ distance
        distance, bit = distance // 2, bit + 1
    return me


def first_kernel(factor, me_ref, atoms_ref, codes_ref, signal_ref, taps_out, part_out, sums_ref):
    slabs, owned, width = codes_ref.shape
    taps = stacked_taps(atoms_ref[...].astype(BF16))
    taps_out[...] = taps
    zero = jnp.zeros((owned, width), BF16)

    def slab_of(n):
        if isinstance(n, int):
            return codes_ref[n] if n >= 0 else zero
        return jnp.where(n >= 0, codes_ref[jnp.maximum(n, 0)], zero)

    rebuild(taps, slab_of, slabs, width, sums_ref)
    partial_residual(me_ref[0], factor, signal_ref, sums_ref, part_out)


def whole_residual(terms):
    rows = terms[0].shape[0] // 2
    mine, other = (ref[:rows, :].astype(F32) + ref[rows:, :].astype(F32) for ref in terms)
    return mine + other


def round_rows(residual, rows_ref):
    count = residual.shape[0]
    rows_ref[:count, :] = residual.astype(BF16).astype(F32)
    rows_ref[count:, :] = jnp.zeros((rows_ref.shape[0] - count, LANES), F32)


def kept_at(piece, slabs, per):
    lane = piece % per * LANES
    return slabs + 3 + piece // per, slice(lane, lane + LANES)


def second_kernel(
    factor, me_ref, sent_ref, other_ref, atoms_ref, codes_ref, thresholds_ref, signal_ref,
    taps_out, codes_out, part_out,
    rows_ref, turned_rows_ref, hankel_ref, gradient_ref, sums_ref,
):
    slabs, owned, width = codes_ref.shape
    per = width // LANES
    round_rows(whole_residual((sent_ref, other_ref)), rows_ref)
    turn_rows(rows_ref, turned_rows_ref, hankel_ref.shape[0] + 1)
    atoms = atoms_ref[...]
    atoms_b = atoms.astype(BF16)
    cutoff = CODE_STEP * thresholds_ref[...]
    gradient_ref[...] = jnp.zeros_like(gradient_ref)
    codes_out[0] = jnp.zeros((owned, width), BF16)

    def body(n):
        frames = windows_of(hankel_ref, n, width)
        code = codes_ref[n]
        both = dot(jnp.concatenate([atoms_b, code], axis=0), frames, ((1,), (0,)))
        gradient_ref[...] += both[owned:]
        value = code.astype(F32) + (CODE_STEP * factor) * both[:owned]
        codes_out[n + 1] = soft(value, cutoff).astype(BF16)

    over_slabs(turned_rows_ref, hankel_ref, slabs, per, body)
    for m in range(2 * per - 1):
        block = hankel_ref[me_ref[0] * per + m]
        for h in range(LANES // owned):
            slab, lane = kept_at(m * (LANES // owned) + h, slabs, per)
            codes_out[slab, :, lane] = block[h * owned : (h + 1) * owned, :]
    after = normalised(atoms + factor * gradient_ref[...])
    after_b = after.astype(BF16)
    codes_out[slabs + 1] = after_b
    codes_out[slabs + 2] = (after - after_b.astype(F32)).astype(BF16)
    taps = stacked_taps(after_b)
    taps_out[...] = taps
    rebuild(taps, lambda n: codes_out[n + 1], slabs, width, sums_ref)
    partial_residual(me_ref[0], factor, signal_ref, sums_ref, part_out)


def atoms_at(ref, places, owned, reach):
    taps = [[ref[(b * reach + p) * owned : (b * reach + p + 1) * owned, :] for p in range(reach)] for b in places]
    return jnp.concatenate([jnp.concatenate(row, axis=1) for row in taps], axis=0)


def rows_at(me, first, places, owned, count):
    return [pl.ds(pl.multiple_of(owner_of(me, first + b, count) * owned, owned), owned) for b in places]


def batches(each, owned):
    together = max(1, min(each, 256 // owned))
    return [range(start, start + together) for start in range(0, each, together)]


def spread(thresholds_ref, cutoffs_ref):
    count = thresholds_ref.shape[0]
    filled = jnp.concatenate([thresholds_ref[...], jnp.zeros((LANES - count, LANES), F32)], axis=0)
    columns = CODE_STEP * filled.T
    for m in range(count):
        cutoffs_ref[m * LANES : (m + 1) * LANES, :] = columns[:, m : m + 1]


def shrink_kernel(factor, owned, me_ref, kept_ref, codes_ref, thresholds_ref, *refs):
    buffers, values_out, cutoffs_ref = refs[:-2], refs[-2], refs[-1]
    atom_count, width = codes_ref.shape
    slabs, per, reach = atom_count // owned, width // LANES, width // LANES
    spread(thresholds_ref, cutoffs_ref)
    each = LANES // owned
    pieces = [kept_at(piece, slabs, per) for piece in range((2 * per - 1) * each)]
    pieces = [kept_ref[slab, :, lane] for slab, lane in pieces]
    frames = windows_of([jnp.concatenate(pieces[i : i + each], axis=0) for i in range(0, len(pieces), each)], 0, width)
    each = slabs // len(buffers)
    for i, ref in enumerate(buffers):
        for places in batches(each, owned):
            there = rows_at(me_ref[0], i * each, places, owned, slabs)
            value = jnp.concatenate([codes_ref[own, :] for own in there], axis=0).astype(F32)
            cutoff = jnp.concatenate([cutoffs_ref[own, :] for own in there], axis=0)
            value += (CODE_STEP * factor) * dot(atoms_at(ref, places, owned, reach), frames, ((1,), (0,)))
            first = (i * each + places[0]) * owned
            values_out[first : first + value.shape[0], :] = soft(value, cutoff).astype(values_out.dtype)


def third_kernel(factor, me_ref, sent_ref, other_ref, kept_ref, values_ref, thresholds_ref, *refs):
    buffers = refs[:-8]
    atoms_out, residual_out, codes_out, rows_ref, turned_rows_ref, hankel_ref, gradient_ref, cutoffs_ref = refs[-8:]
    owned, lag_count = atoms_out.shape
    atom_count, width = values_ref.shape
    slabs, per, reach = atom_count // owned, width // LANES, lag_count // LANES
    me = me_ref[0]
    residual = whole_residual((sent_ref, other_ref))
    round_rows(residual, rows_ref)
    turn_rows(rows_ref, turned_rows_ref, hankel_ref.shape[0] + 1)
    spread(thresholds_ref, cutoffs_ref)
    gradient_ref[...] = jnp.zeros_like(gradient_ref)

    def body(n):
        blocks = [hankel_ref[n * per + i] for i in range(per)]
        gradient_ref[...] += dot(delayed(kept_ref[n + 1], kept_ref[n]), jnp.concatenate(blocks, axis=0), ((1,), (0,)))

    over_slabs(turned_rows_ref, hankel_ref, slabs, per, body)
    gradient = jnp.concatenate([gradient_ref[p * owned : (p + 1) * owned, :] for p in range(reach)], axis=1)
    atoms = kept_ref[slabs + 1].astype(F32) + kept_ref[slabs + 2].astype(F32)
    atoms_out[...] = normalised(atoms + factor * gradient)
    rows_ref[: slabs * per, :] = residual
    residual_out[...] = rows_ref[pl.ds(me * per, per), :]
    frames = windows_of(hankel_ref, me, width)
    each = slabs // len(buffers)
    for i, ref in enumerate(buffers):
        for places in batches(each, owned):
            there = rows_at(me, i * each, places, owned, slabs)
            cutoff = jnp.concatenate([cutoffs_ref[own, :] for own in there], axis=0)
            change = (CODE_STEP * factor) * dot(atoms_at(ref, places, owned, reach), frames, ((1,), (0,)))
            first = (i * each + places[0]) * owned
            value = soft(values_ref[first : first + change.shape[0], :].astype(F32) + change, cutoff).astype(BF16)
            for b, own in enumerate(there):
                codes_out[own, :] = value[b * owned : (b + 1) * owned]


def call(kernel, outs, scratch, *args):
    vmem = pl.BlockSpec(memory_space=pltpu.VMEM)
    room = sum(math.prod(a.shape) * jnp.dtype(a.dtype).itemsize for a in [*args, *outs, *scratch])
    return pl.pallas_call(
        kernel,
        out_shape=tuple(outs),
        in_specs=[pl.BlockSpec(memory_space=pltpu.SMEM)] + [vmem] * (len(args) - 1),
        out_specs=(vmem,) * len(outs),
        scratch_shapes=scratch,
        compiler_params=pltpu.CompilerParams(vmem_limit_bytes=room + 14 * 1024 * 1024),
    )(*args)


def swapped(block, distance):
    count = lax.axis_size("tm")
    return lax.ppermute(block, "tm", [(i, i ^ distance) for i in range(count)])


def tied(value, *others):
    return lax.optimization_barrier((value, others))[0]


def exchanged(block, part, alone, late={}):
    distance = lax.axis_size("tm") // 2
    rows = part.shape[0]
    buffers = [block]
    while True:
        high = lax.reduce_precision(part, 8, 7)
        low = lax.reduce_precision(part - high, 8, 7)
        sent = [high.astype(BF16), low.astype(BF16)]
        if distance > alone:
            sent = buffers + sent
        sent = jnp.concatenate(sent)
        if distance in late:
            sent = tied(sent, late[distance])
        other = swapped(sent, distance)
        end = sent.shape[0] - 2 * rows
        if distance > alone:
            buffers = [sent[:end], other[:end]]
            whole = [sent, other]
        if distance == 1:
            return buffers, whole, (sent, other)
        part = (high + low) + (other[end : end + rows].astype(F32) + other[end + rows :].astype(F32))
        distance //= 2


def on_device(signal, codes, dictionary, thresholds):
    _, atom_count, width = codes.shape
    owned, lag_count = dictionary.shape
    slabs = lax.axis_size("tm")
    per = width // LANES
    blocks = slabs * per
    factor = (atom_count * lag_count) ** (-0.5)
    me = lax.axis_index("tm")
    at = me.astype(jnp.int32).reshape(1)
    signal_rows = signal.reshape(per, LANES)
    own_thresholds = lax.dynamic_slice(thresholds, (me * owned,), (owned,)).reshape(owned, 1)
    codes = codes[0]

    by_atom = lax.all_to_all(codes.reshape(slabs, owned, width), "tm", 0, 0, tiled=True)

    sums = [pltpu.VMEM((blocks, 8, LANES), F32)]
    windows = [
        pltpu.VMEM((blocks + 8, LANES), F32),
        pltpu.VMEM((blocks + 8, 8, LANES), F32),
        pltpu.VMEM((blocks + per - 1, LANES, LANES), BF16),
        pltpu.VMEM((owned, lag_count), F32),
    ]
    atoms_shape = jax.ShapeDtypeStruct((owned, lag_count), F32)
    taps_shape = jax.ShapeDtypeStruct((owned * lag_count // LANES, LANES), BF16)
    part_shape = jax.ShapeDtypeStruct((blocks, LANES), F32)
    taps, part = call(
        functools.partial(first_kernel, factor), (taps_shape, part_shape), sums, at, dictionary, by_atom, signal_rows
    )
    before, _, first = exchanged(taps, part, 2)
    kept = slabs + 3 + pl.cdiv((2 * per - 1) * (LANES // owned), per)
    taps, kept, part = call(
        functools.partial(second_kernel, factor),
        [taps_shape, jax.ShapeDtypeStruct((kept, owned, width), BF16), part_shape],
        windows + sums,
        at, *first, dictionary, by_atom, own_thresholds, signal_rows,
    )
    all_thresholds = thresholds.reshape(-1, LANES)
    cutoffs = pltpu.VMEM((atom_count, 1), F32)
    mine = jnp.concatenate(before)
    other = swapped(tied(mine, part), 2)
    before = [mine, other, swapped(mine, 1), swapped(other, 1)]
    (values,) = call(
        functools.partial(shrink_kernel, factor, owned),
        [jax.ShapeDtypeStruct((atom_count, width), F32)],
        [cutoffs],
        at, kept, codes, all_thresholds, *before,
    )
    _, after, second = exchanged(taps, part, 1, {4: other, 1: values})
    after = after + [swapped(buffer, 1) for buffer in after]
    atoms, residual, codes = call(
        functools.partial(third_kernel, factor),
        [
            atoms_shape,
            jax.ShapeDtypeStruct((per, LANES), F32),
            jax.ShapeDtypeStruct((atom_count, width), BF16),
        ],
        [*windows[:-1], pltpu.VMEM(taps_shape.shape, F32), cutoffs],
        at, *second, kept, values, all_thresholds, *after,
    )
    return codes[None], atoms, residual.reshape(1, width)


def solution(mesh):
    return jax.shard_map(
        on_device,
        mesh=mesh,
        in_specs=(P("groups", "tm"), P("groups", None, "tm"), P("tm", None), P()),
        out_specs=(P("groups", None, "tm"), P(("groups", "tm"), None), P("groups", "tm")),
        check_vma=False,
    )
```
